128 devices in a mesh: gx: 8 (over z, x_lo), gy: 16 (over y, x_hi, core).
Axes of the slice: x: 4 (x_hi: 2, x_lo: 2; x = x_hi * 2 + x_lo), y: 4, z: 4, core: 2. Of those that a mesh axis runs over, the one named last changes fastest.
Arguments:
- picture_raw_features: bfloat16 [65536, 1152], P(('gx', 'gy')), may hold values from -0.54 to 0.54
- caption_raw_features: bfloat16 [65536, 1152], P(('gx', 'gy')), may hold values from -0.54 to 0.54
- peer_assignment: int32 [3, 128], replicated, may hold values from 0 to 127, as said below
- sharpness_factor: float32 [1], replicated, may hold values from 4 to 16
- offset_term: float32 [1], replicated, may hold values from -3 to -0.5
Outputs:
- image_embedding_gradient: float32 [65536, 1152], P(('gx', 'gy'))
- grad_text: float32 [65536, 1152], P(('gx', 'gy'))
- row_loss: float32 [65536], P(('gx', 'gy'))
The draws below stay inside these ranges and needn't reach their ends.
Inputs may be any that keep to these rules, and one draw needn't show every extreme that they name: `peer_assignment`: row r maps device i to (i + s_r) mod 128 for an offset s_r of 1 to 127; the offsets of the 3 rounds differ.
All inputs are finite; a program needn't handle non-finite values.
Results may differ from the reference program's by a relative error of at most 0.005.
Values may be sent and summed in bfloat16 or wider, within the bound.
No kernel may reach another device: no remote copies, remote signals or barrier semaphores. Data moves between devices by JAX's collectives and lax.ppermute only.
A program may use at most 192 MiB of HBM per device.

```python
import math
import jax
import jax.numpy as jnp
from jax import lax

D = 1152
ROWS = 512
ROUNDS = 3
TOKENS = 65536


def draw_picture_raw_features(key, part):
    key = jax.random.fold_in(key, 3)
    first_key, second_key = jax.random.split(key)
    base = jnp.clip(jax.random.normal(first_key, (TOKENS, D), jnp.float32), -6.0, 6.0)
    spread = jnp.exp(jax.random.uniform(second_key, (TOKENS, 1), jnp.float32, math.log(0.3), math.log(3.0)))
    return (0.03 * base * spread).astype(jnp.bfloat16)


def draw_caption_raw_features(key, part):
    key = jax.random.fold_in(key, 5)
    first_key, second_key = jax.random.split(key)
    base = jnp.clip(jax.random.normal(first_key, (TOKENS, D), jnp.float32), -6.0, 6.0)
    spread = jnp.exp(jax.random.uniform(second_key, (TOKENS, 1), jnp.float32, math.log(0.3), math.log(3.0)))
    return (0.03 * base * spread).astype(jnp.bfloat16)


def draw_peer_assignment(key, part):
    key = jax.random.fold_in(key, 11)
    device_count = TOKENS // ROWS
    offsets = jax.random.permutation(key, device_count - 1)[:ROUNDS].astype(jnp.int32) + 1
    indices = jnp.arange(device_count, dtype=jnp.int32)
    return (indices[None, :] + offsets[:, None]) % device_count


def setup_inputs(seed: int = 0) -> dict:
    streams_of = jax.random.split(jax.random.key(seed), 6)
    picture_raw_features = draw_picture_raw_features(jax.random.fold_in(streams_of[5], 71), 0)
    caption_raw_features = draw_caption_raw_features(jax.random.fold_in(streams_of[5], 71), 0)
    peer_assignment = draw_peer_assignment(jax.random.fold_in(streams_of[5], 71), 0)
    sharpness_factor = jnp.clip(jnp.exp(jax.random.uniform(streams_of[3], (1,), jnp.float32, math.log(4.0), math.log(16.0))), 4.0, 16.0)
    offset_term = jnp.clip(jax.random.uniform(streams_of[4], (1,), jnp.float32, -3.0, -0.5), -3.0, -0.5)
    return dict(picture_raw_features=picture_raw_features, caption_raw_features=caption_raw_features, peer_assignment=peer_assignment, sharpness_factor=sharpness_factor, offset_term=offset_term)


def normalize(raw):
    widened = raw.astype(jnp.float32)
    scaling_multiplier = lax.rsqrt(lax.optimization_barrier(jnp.sum(widened * widened, axis=-1, keepdims=True)) + 1e-06)
    return (widened, scaling_multiplier, (widened * scaling_multiplier).astype(jnp.bfloat16))

def restore(widened, scaling_multiplier, unit_grad):
    inner_prod = lax.optimization_barrier(jnp.sum(widened * unit_grad, axis=-1, keepdims=True))
    return scaling_multiplier * unit_grad - widened * (scaling_multiplier * scaling_multiplier * scaling_multiplier) * inner_prod

def rounded(value):
    return lax.optimization_barrier(value.astype(jnp.bfloat16)).astype(jnp.float32)

def reference(picture_raw_features, caption_raw_features, peer_assignment, sharpness_factor, offset_term):
    score_sharpness = sharpness_factor[0]
    score_offset = offset_term[0]
    image_wide, image_factor, picture_normed = normalize(picture_raw_features)
    text_wide, text_factor, caption_normed = normalize(caption_raw_features)
    block_count = TOKENS // ROWS
    picture_groups = picture_normed.reshape(block_count, ROWS, D).astype(jnp.float32)
    caption_groups = caption_normed.reshape(block_count, ROWS, D).astype(jnp.float32)
    matched_mask = jnp.eye(ROWS, dtype=jnp.float32)
    local_scores = score_sharpness * jnp.einsum('rbw,rxw->rbx', picture_groups, caption_groups) + score_offset
    loss_rows = lax.optimization_barrier(jnp.sum(jax.nn.softplus(local_scores) - matched_mask * local_scores, axis=-1))
    local_factor = (score_sharpness * (jax.nn.sigmoid(local_scores) - matched_mask)).astype(jnp.bfloat16).astype(jnp.float32)
    image_grad = jnp.einsum('naj,njd->nad', local_factor, caption_groups)
    text_grad = jnp.einsum('naj,nad->njd', local_factor, picture_groups)
    for round_index in range(ROUNDS):
        partners = peer_assignment[round_index].astype(jnp.int32)
        offset = partners[0].astype(jnp.int32)
        peer_caption_entries = caption_groups[partners]
        score_matrix = score_sharpness * jnp.einsum('rbw,rxw->rbx', picture_groups, peer_caption_entries) + score_offset
        loss_rows = loss_rows + lax.optimization_barrier(jnp.sum(jax.nn.softplus(score_matrix), axis=-1))
        weight_factor = (score_sharpness * jax.nn.sigmoid(score_matrix)).astype(jnp.bfloat16).astype(jnp.float32)
        image_grad = image_grad + rounded(jnp.einsum('naj,njd->nad', weight_factor, peer_caption_entries))
        sent_parts = rounded(jnp.einsum('naj,nad->njd', weight_factor, picture_groups))
        text_grad = text_grad + jnp.roll(sent_parts, offset, axis=0)
    image_embedding_gradient = restore(image_wide, image_factor, image_grad.reshape(TOKENS, D))
    grad_text = restore(text_wide, text_factor, text_grad.reshape(TOKENS, D))
    row_loss = loss_rows.reshape(TOKENS) / ((ROUNDS + 1) * ROWS)
    return (image_embedding_gradient, grad_text, row_loss)
```

```python
import functools
import itertools

import jax
import jax.numpy as jnp
from jax import lax
from jax.experimental import pallas as pl
from jax.experimental.pallas import tpu as pltpu
from jax.sharding import PartitionSpec as P

AXES = ("gx", "gy")
HALF = 256
LANES = 128

STEP_COST = (
    0, 35, 59, 38, 42, 53, 80, 66, 69, 54, 70, 58, 55, 48, 63, 43, 62, 40, 66, 43, 58, 54, 74, 66, 69, 59, 73, 56, 48,
    42, 65, 36, 39, 49, 67, 59, 61, 65, 76, 63, 70, 65, 78, 69, 76, 69, 77, 68, 76, 72, 79, 70, 80, 69, 81, 64, 71, 67,
    77, 67, 69, 65, 72, 64, 62,
)


def trees():
    edges = list(itertools.combinations(range(4), 2))
    found = []
    for chosen in itertools.combinations(edges, 3):
        reached, steps = [0], []
        while len(reached) < 4:
            more = [(a, b) for a, b in chosen if (a in reached) != (b in reached)]
            if not more:
                break
            a, b = more[0]
            if b in reached:
                a, b = b, a
            steps.append((reached.index(a), a, b))
            reached.append(b)
        if len(reached) == 4:
            found.append((chosen, steps))
    return edges, found


EDGES, TREES = trees()


def plan_kernel(device_count, peers, cost, out):
    node = [jnp.int32(0), peers[0, 0], peers[1, 0], peers[2, 0]]

    def apart(a, b):
        gap = node[b] - node[a]
        return jnp.where(gap < 0, gap + device_count, gap)

    weight = {}
    for a, b in EDGES:
        gap = apart(a, b)
        weight[a, b] = cost[jnp.minimum(gap, device_count - gap)]
    best = None
    for chosen, steps in TREES:
        total = sum(weight[e] for e in chosen)
        fields = []
        for slot, a, b in steps:
            fields += [jnp.int32(slot), apart(a, b)]
        if best is None:
            best, kept = total, fields
        else:
            better = total < best
            best = jnp.where(better, total, best)
            kept = [jnp.where(better, n, o) for n, o in zip(fields, kept)]
    for place, value in enumerate(kept):
        out[place] = value


def make_plan(peers, device_count):
    smem = pl.BlockSpec(memory_space=pltpu.SMEM)
    return pl.pallas_call(
        functools.partial(plan_kernel, device_count),
        out_shape=jax.ShapeDtypeStruct((6,), jnp.int32),
        in_specs=[smem, smem],
        out_specs=smem,
        name="plan",
    )(peers, jnp.array(STEP_COST, jnp.int32))


def shifted(x, by, size):
    return lax.ppermute(x, AXES, [(i, (i + by) % size) for i in range(size)])


def move(texts, images, offset, size):
    def mover(by):
        return lambda t, i: (shifted(t, -by, size), shifted(i, by, size))

    return lax.switch(offset - 1, [mover(by) for by in range(1, size)], texts, images)


def norm_kernel(pic, cap, unit_pic, unit_cap, pic_factor, cap_factor):
    for raw, unit, factor in ((pic, unit_pic, pic_factor), (cap, unit_cap, cap_factor)):
        wide = raw[...].astype(jnp.float32)
        scale = lax.rsqrt(jnp.sum(wide * wide, axis=-1, keepdims=True) + 1e-06)
        unit[...] = (wide * scale).astype(jnp.bfloat16)
        factor[...] = scale


def normalize(pic, cap):
    rows, width = pic.shape
    block = pl.BlockSpec((HALF, width), lambda i: (i, 0))
    column = pl.BlockSpec((HALF, 1), lambda i: (i, 0))
    unit = jax.ShapeDtypeStruct((rows, width), jnp.bfloat16)
    factor = jax.ShapeDtypeStruct((rows, 1), jnp.float32)
    return pl.pallas_call(
        norm_kernel,
        grid=(rows // HALF,),
        out_shape=(unit, unit, factor, factor),
        in_specs=[block, block],
        out_specs=(block, block, column, column),
        name="normalize",
    )(pic, cap)


def scores(left, right, sharp, shift):
    dots = lax.dot_general(left, right, (((1,), (1,)), ((), ())), preferred_element_type=jnp.float32)
    return sharp * dots + shift


def folded(wide):
    return sum(wide[:, k : k + LANES] for k in range(0, wide.shape[1], LANES))


def product(coeff, entries):
    return lax.dot_general(coeff, entries, (((1,), (0,)), ((), ())), preferred_element_type=jnp.float32)


def own_kernel(sharp, shift, pic, cap, all_pic, all_cap, pic_grad, cap_grad, loss):
    first = pl.program_id(0) * HALF
    columns = all_pic.shape[0]
    rows_at = lax.broadcasted_iota(jnp.int32, (HALF, columns), 0) + first
    columns_at = lax.broadcasted_iota(jnp.int32, (HALF, columns), 1)
    label = jnp.where(rows_at == columns_at, 1.0, 0.0)
    for left, right, grad in ((pic, all_cap, pic_grad), (cap, all_pic, cap_grad)):
        logits = scores(left[...], right[...], sharp[0], shift[0])
        odds = jnp.exp(logits)
        if left is pic:
            loss[...] = folded(jnp.log1p(odds) - label * logits)
        coeff = (sharp[0] * (odds / (1.0 + odds) - label)).astype(jnp.bfloat16)
        grad[...] = product(coeff, right[...])


def cross_parts(sharp, shift, pic, cap, peer_pic, peer_cap):
    logits = scores(pic[...], peer_cap[...], sharp[0], shift[0])
    odds = jnp.exp(logits)
    loss = folded(jnp.log1p(odds))
    coeff = (sharp[0] * (odds / (1.0 + odds))).astype(jnp.bfloat16)
    pic_part = product(coeff, peer_cap[...]).astype(jnp.bfloat16).astype(jnp.float32)
    logits = scores(cap[...], peer_pic[...], sharp[0], shift[0])
    odds = jnp.exp(logits)
    coeff = (sharp[0] * (odds / (1.0 + odds))).astype(jnp.bfloat16)
    cap_part = product(coeff, peer_pic[...]).astype(jnp.bfloat16).astype(jnp.float32)
    return pic_part, cap_part, loss


def cross_kernel(sharp, shift, pic, cap, peer_pic, peer_cap, pic_sum, cap_sum, loss_sum, pic_grad, cap_grad, loss):
    pic_part, cap_part, loss_part = cross_parts(sharp, shift, pic, cap, peer_pic, peer_cap)
    pic_grad[...] = pic_sum[...] + pic_part
    cap_grad[...] = cap_sum[...] + cap_part
    loss[...] = loss_sum[...] + loss_part


def restored(raw, factor, grad):
    wide = raw[...].astype(jnp.float32)
    scale = factor[...]
    inner = jnp.sum(wide * grad, axis=-1, keepdims=True)
    return scale * grad - wide * (scale * scale * scale * inner)


def last_kernel(
    mean_of, sharp, shift, pic, cap, peer_pic, peer_cap, pic_sum, cap_sum, loss_sum,
    raw_pic, raw_cap, pic_factor, cap_factor, pic_grad, cap_grad, loss,
):
    pic_part, cap_part, loss_part = cross_parts(sharp, shift, pic, cap, peer_pic, peer_cap)
    pic_grad[...] = restored(raw_pic, pic_factor, pic_sum[...] + pic_part)
    cap_grad[...] = restored(raw_cap, cap_factor, cap_sum[...] + cap_part)
    ones = jnp.full((8, LANES), 1.0, jnp.float32)
    total = lax.dot_general(
        ones, loss_sum[...] + loss_part, (((1,), (1,)), ((), ())),
        precision=lax.Precision.HIGHEST, preferred_element_type=jnp.float32,
    )
    loss[...] = total[0:1, :] * (1.0 / mean_of)


def specs(rows, width):
    smem = pl.BlockSpec(memory_space=pltpu.SMEM)
    block = pl.BlockSpec((HALF, width), lambda i: (i, 0))
    whole = pl.BlockSpec((rows, width), lambda i: (0, 0))
    lanes = pl.BlockSpec((HALF, LANES), lambda i: (i, 0))
    column = pl.BlockSpec((HALF, 1), lambda i: (i, 0))
    return smem, block, whole, lanes, column


def params(rows, width, products):
    return dict(
        compiler_params=pltpu.CompilerParams(vmem_limit_bytes=40 * 2**20),
        cost_estimate=pl.CostEstimate(
            flops=2 * products * rows * rows * width, bytes_accessed=20 * rows * width, transcendentals=4 * rows * rows
        ),
    )


def own_tile(sharp, shift, pic, cap):
    rows, width = pic.shape
    smem, block, whole, lanes, column = specs(rows, width)
    wide = jax.ShapeDtypeStruct((rows, width), jnp.float32)
    return pl.pallas_call(
        own_kernel,
        grid=(rows // HALF,),
        out_shape=(wide, wide, jax.ShapeDtypeStruct((rows, LANES), jnp.float32)),
        in_specs=[smem, smem, block, block, whole, whole],
        out_specs=(block, block, lanes),
        name="own_tile",
        **params(rows, width, 4),
    )(sharp, shift, pic, cap, pic, cap)


def cross_tile(sharp, shift, pic, cap, peer_pic, peer_cap, sums):
    rows, width = pic.shape
    smem, block, whole, lanes, column = specs(rows, width)
    wide = jax.ShapeDtypeStruct((rows, width), jnp.float32)
    return pl.pallas_call(
        cross_kernel,
        grid=(rows // HALF,),
        out_shape=(wide, wide, jax.ShapeDtypeStruct((rows, LANES), jnp.float32)),
        in_specs=[smem, smem, block, block, whole, whole, block, block, lanes],
        out_specs=(block, block, lanes),
        input_output_aliases={6: 0, 7: 1, 8: 2},
        name="cross_tile",
        **params(rows, width, 4),
    )(sharp, shift, pic, cap, peer_pic, peer_cap, *sums)


def last_tile(mean_of, sharp, shift, pic, cap, peer_pic, peer_cap, sums, raw_pic, raw_cap, pic_factor, cap_factor):
    rows, width = pic.shape
    smem, block, whole, lanes, column = specs(rows, width)
    wide = jax.ShapeDtypeStruct((rows, width), jnp.float32)
    return pl.pallas_call(
        functools.partial(last_kernel, mean_of),
        grid=(rows // HALF,),
        out_shape=(wide, wide, jax.ShapeDtypeStruct((1, rows), jnp.float32)),
        in_specs=[smem, smem, block, block, whole, whole, block, block, lanes, block, block, column, column],
        out_specs=(block, block, pl.BlockSpec((1, HALF), lambda i: (0, i))),
        input_output_aliases={6: 0, 7: 1},
        name="last_tile",
        **params(rows, width, 4),
    )(sharp, shift, pic, cap, peer_pic, peer_cap, *sums, raw_pic, raw_cap, pic_factor, cap_factor)


def pick(slot, choices):
    picked = choices[0]
    for place in range(1, len(choices)):
        picked = jnp.where(slot == place, choices[place], picked)
    return picked


def shards(picture_raw_features, caption_raw_features, peer_assignment, sharpness_factor, offset_term):
    size = peer_assignment.shape[1]
    rows = picture_raw_features.shape[0]
    plan = make_plan(peer_assignment, size)
    pic, cap, pic_factor, cap_factor = normalize(picture_raw_features, caption_raw_features)
    images, texts = [pic], [cap]
    sums = own_tile(sharpness_factor, offset_term, pic, cap)
    for step in range(3):
        slot, offset = plan[2 * step], plan[2 * step + 1]
        peer_cap, peer_pic = move(pick(slot, texts), pick(slot, images), offset, size)
        texts.append(peer_cap)
        images.append(peer_pic)
        if step < 2:
            sums = cross_tile(sharpness_factor, offset_term, pic, cap, peer_pic, peer_cap, sums)
    image_embedding_gradient, grad_text, row_loss = last_tile(
        4 * rows, sharpness_factor, offset_term, pic, cap, peer_pic, peer_cap, sums,
        picture_raw_features, caption_raw_features, pic_factor, cap_factor,
    )
    return image_embedding_gradient, grad_text, row_loss.reshape(rows)


def solution(mesh):
    placed = (P(AXES, None), P(AXES, None), P(), P(), P())
    return jax.shard_map(
        shards,
        mesh=mesh,
        in_specs=placed,
        out_specs=(P(AXES, None), P(AXES, None), P(AXES)),
        check_vma=False,
    )
```

```python
import functools
import itertools

import jax
import jax.numpy as jnp
from jax import lax
from jax.experimental import pallas as pl
from jax.experimental.pallas import tpu as pltpu
from jax.sharding import PartitionSpec as P

AXES = ("gx", "gy")
HALF = 256
LANES = 128
FIELDS = 6

STEP_COST = (
    0, 35, 59, 38, 42, 53, 80, 66, 69, 54, 70, 58, 55, 48, 63, 43, 62, 40, 66, 43, 58, 54, 74, 66, 69, 59, 73, 56, 48,
    42, 65, 36, 39, 49, 67, 59, 61, 65, 76, 63, 70, 65, 78, 69, 76, 69, 77, 68, 76, 72, 79, 70, 80, 69, 81, 64, 71, 67,
    77, 67, 69, 65, 72, 64, 62,
)


def trees():
    edges = list(itertools.combinations(range(4), 2))
    found = []
    for chosen in itertools.combinations(edges, 3):
        reached, steps = [0], []
        while len(reached) < 4:
            more = [(a, b) for a, b in chosen if (a in reached) != (b in reached)]
            if not more:
                break
            a, b = more[0]
            if b in reached:
                a, b = b, a
            steps.append((reached.index(a), a, b))
            reached.append(b)
        if len(reached) == 4:
            found.append((chosen, steps))
    return edges, found


EDGES, TREES = trees()


def plan(peers, cost, out):
    size = peers.shape[1]
    node = [jnp.int32(0), peers[0, 0], peers[1, 0], peers[2, 0]]

    def apart(a, b):
        gap = node[b] - node[a]
        return jnp.where(gap < 0, gap + size, gap)

    weight = {}
    for a, b in EDGES:
        gap = apart(a, b)
        weight[a, b] = cost[jnp.minimum(gap, size - gap)]
    best = None
    for chosen, steps in TREES:
        total = sum(weight[e] for e in chosen)
        fields = []
        for slot, a, b in steps:
            fields += [jnp.int32(slot), apart(a, b)]
        if best is None:
            best, kept = total, fields
        else:
            better = total < best
            best = jnp.where(better, total, best)
            kept = [jnp.where(better, n, o) for n, o in zip(fields, kept)]
    swaps = [jnp.int32(0)]
    for step in range(3):
        slot, gap = kept[2 * step], kept[2 * step + 1]
        swap = jnp.where(gap > size // 2, 1, 0)
        held = sum(jnp.where(slot == k, swaps[k], 0) for k in range(step + 1))
        branch = jnp.minimum(gap, size - gap) - 1
        crossed = jnp.where(swap == held, 0, 1)
        out[FIELDS * step] = 2 * slot + crossed
        out[FIELDS * step + 1] = 2 * slot + 1 - crossed
        out[FIELDS * step + 2] = branch // 16
        out[FIELDS * step + 3] = branch // 4 % 4
        out[FIELDS * step + 4] = branch % 4
        out[FIELDS * step + 5] = swap
        swaps.append(swap)
    return swaps[1]


def start_kernel(peers, cost, raw_pic, raw_cap, steps, pic, cap, ahead, behind, pic_factor, cap_factor):
    swap = plan(peers, cost, steps)
    units = []
    for raw, unit, factor in ((raw_pic, pic, pic_factor), (raw_cap, cap, cap_factor)):
        wide = raw[...].astype(jnp.float32)
        scale = lax.rsqrt(jnp.sum(wide * wide, axis=-1, keepdims=True) + 1e-06)
        units.append((wide * scale).astype(jnp.bfloat16))
        unit[...] = units[-1]
        factor[...] = scale
    ahead[...] = jnp.where(swap == 1, units[0], units[1])
    behind[...] = jnp.where(swap == 1, units[1], units[0])


def start(peers, pic, cap):
    rows, width = pic.shape
    smem, block, whole, lanes, column = specs(rows, width)
    unit = jax.ShapeDtypeStruct((rows, width), jnp.bfloat16)
    factor = jax.ShapeDtypeStruct((rows, 1), jnp.float32)
    return pl.pallas_call(
        start_kernel,
        grid=(rows // HALF,),
        out_shape=(jax.ShapeDtypeStruct((3 * FIELDS,), jnp.int32), unit, unit, unit, unit, factor, factor),
        in_specs=[smem, smem, block, block],
        out_specs=(smem, block, block, block, block, column, column),
        name="start",
    )(peers, jnp.array(STEP_COST, jnp.int32), pic, cap)


def shifted(x, by, size):
    return lax.ppermute(x, AXES, [(i, (i + by) % size) for i in range(size)])


def step_branches(digits, size, compute, operands):
    def branch(by):
        def run(ahead, behind, *rest):
            arrived = shifted(ahead, -by, size), shifted(behind, by, size)
            return *arrived, *compute(*rest)

        return run

    def middle(high, mid):
        return lambda low, *rest: lax.switch(low, [branch(16 * high + 4 * mid + k + 1) for k in range(4)], *rest)

    def outer(high):
        return lambda mid, low, *rest: lax.switch(mid, [middle(high, k) for k in range(4)], low, *rest)

    return lax.switch(digits[0], [outer(k) for k in range(4)], digits[1], digits[2], *operands)


def scores(left, right, sharp, shift):
    dots = lax.dot_general(left, right, (((1,), (1,)), ((), ())), preferred_element_type=jnp.float32)
    return sharp * dots + shift


def odds_ratio(odds):
    total = 1.0 + odds
    guess = pl.reciprocal(total, approx=True)
    return odds * (guess * (2.0 - total * guess))


def log_total(odds):
    return jnp.where(odds < 1e-3, odds - 0.5 * odds * odds, jnp.log(1.0 + odds))


def folded(wide):
    return sum(wide[:, k : k + LANES] for k in range(0, wide.shape[1], LANES))


def product(coeff, entries):
    return lax.dot_general(coeff, entries, (((1,), (0,)), ((), ())), preferred_element_type=jnp.float32)


def own_kernel(sharp, shift, pic, cap, all_pic, all_cap, pic_grad, cap_grad, loss):
    first = pl.program_id(0) * HALF
    columns = all_pic.shape[0]
    rows_at = lax.broadcasted_iota(jnp.int32, (HALF, columns), 0) + first
    columns_at = lax.broadcasted_iota(jnp.int32, (HALF, columns), 1)
    label = jnp.where(rows_at == columns_at, 1.0, 0.0)
    for left, right, grad in ((pic, all_cap, pic_grad), (cap, all_pic, cap_grad)):
        logits = scores(left[...], right[...], sharp[0], shift[0])
        odds = jnp.exp(logits)
        if left is pic:
            loss[...] = folded(log_total(odds) - label * logits)
        coeff = (sharp[0] * (odds_ratio(odds) - label)).astype(jnp.bfloat16)
        grad[...] = product(coeff, right[...])


def sort_peers(swap, ahead, behind, peer_pic, peer_cap):
    @pl.when(pl.program_id(0) == 0)
    def _():
        peer_cap[...] = jnp.where(swap == 1, behind[...], ahead[...])
        peer_pic[...] = jnp.where(swap == 1, ahead[...], behind[...])


def cross_parts(sharp, shift, pic, cap, peer_pic, peer_cap):
    logits = scores(pic[...], peer_cap[...], sharp[0], shift[0])
    odds = jnp.exp(logits)
    loss = folded(log_total(odds))
    coeff = (sharp[0] * odds_ratio(odds)).astype(jnp.bfloat16)
    pic_part = product(coeff, peer_cap[...]).astype(jnp.bfloat16).astype(jnp.float32)
    logits = scores(cap[...], peer_pic[...], sharp[0], shift[0])
    coeff = (sharp[0] * odds_ratio(jnp.exp(logits))).astype(jnp.bfloat16)
    cap_part = product(coeff, peer_pic[...]).astype(jnp.bfloat16).astype(jnp.float32)
    return pic_part, cap_part, loss


def cross_kernel(
    step, steps, sharp, shift, pic, cap, ahead, behind, pic_sum, cap_sum, loss_sum,
    pic_grad, cap_grad, loss, peer_pic, peer_cap,
):
    sort_peers(steps[FIELDS * step + 5], ahead, behind, peer_pic, peer_cap)
    pic_part, cap_part, loss_part = cross_parts(sharp, shift, pic, cap, peer_pic, peer_cap)
    pic_grad[...] = pic_sum[...] + pic_part
    cap_grad[...] = cap_sum[...] + cap_part
    loss[...] = loss_sum[...] + loss_part


def restored(raw, factor, grad):
    wide = raw[...].astype(jnp.float32)
    scale = factor[...]
    inner = jnp.sum(wide * grad, axis=-1, keepdims=True)
    return scale * grad - wide * (scale * scale * scale * inner)


def last_kernel(
    mean_of, step, steps, sharp, shift, pic, cap, ahead, behind, pic_sum, cap_sum, loss_sum,
    raw_pic, raw_cap, pic_factor, cap_factor, pic_grad, cap_grad, loss, peer_pic, peer_cap,
):
    sort_peers(steps[FIELDS * step + 5], ahead, behind, peer_pic, peer_cap)
    pic_part, cap_part, loss_part = cross_parts(sharp, shift, pic, cap, peer_pic, peer_cap)
    pic_grad[...] = restored(raw_pic, pic_factor, pic_sum[...] + pic_part)
    cap_grad[...] = restored(raw_cap, cap_factor, cap_sum[...] + cap_part)
    ones = jnp.full((8, LANES), 1.0, jnp.float32)
    total = lax.dot_general(
        ones, loss_sum[...] + loss_part, (((1,), (1,)), ((), ())),
        precision=lax.Precision.HIGHEST, preferred_element_type=jnp.float32,
    )
    loss[...] = total[0:1, :] * (1.0 / mean_of)


def specs(rows, width):
    smem = pl.BlockSpec(memory_space=pltpu.SMEM)
    block = pl.BlockSpec((HALF, width), lambda i: (i, 0))
    whole = pl.BlockSpec((rows, width), lambda i: (0, 0))
    lanes = pl.BlockSpec((HALF, LANES), lambda i: (i, 0))
    column = pl.BlockSpec((HALF, 1), lambda i: (i, 0))
    return smem, block, whole, lanes, column


def params(rows, width):
    return dict(
        compiler_params=pltpu.CompilerParams(vmem_limit_bytes=40 * 2**20),
        cost_estimate=pl.CostEstimate(
            flops=8 * rows * rows * width, bytes_accessed=20 * rows * width, transcendentals=4 * rows * rows
        ),
    )


def own_tile(sharp, shift, pic, cap):
    rows, width = pic.shape
    smem, block, whole, lanes, column = specs(rows, width)
    wide = jax.ShapeDtypeStruct((rows, width), jnp.float32)
    return pl.pallas_call(
        own_kernel,
        grid=(rows // HALF,),
        out_shape=(wide, wide, jax.ShapeDtypeStruct((rows, LANES), jnp.float32)),
        in_specs=[smem, smem, block, block, whole, whole],
        out_specs=(block, block, lanes),
        name="own_tile",
        **params(rows, width),
    )(sharp, shift, pic, cap, pic, cap)


def cross_tile(step, steps, sharp, shift, pic, cap, ahead, behind, *sums):
    rows, width = pic.shape
    smem, block, whole, lanes, column = specs(rows, width)
    wide = jax.ShapeDtypeStruct((rows, width), jnp.float32)
    return pl.pallas_call(
        functools.partial(cross_kernel, step),
        grid=(rows // HALF,),
        out_shape=(wide, wide, jax.ShapeDtypeStruct((rows, LANES), jnp.float32)),
        in_specs=[smem, smem, smem, block, block, whole, whole, block, block, lanes],
        out_specs=(block, block, lanes),
        scratch_shapes=[pltpu.VMEM((rows, width), jnp.bfloat16)] * 2,
        name="cross_tile",
        **params(rows, width),
    )(steps, sharp, shift, pic, cap, ahead, behind, *sums)


def last_tile(mean_of, step, steps, sharp, shift, pic, cap, ahead, behind, sums, *rest):
    rows, width = pic.shape
    smem, block, whole, lanes, column = specs(rows, width)
    wide = jax.ShapeDtypeStruct((rows, width), jnp.float32)
    return pl.pallas_call(
        functools.partial(last_kernel, mean_of, step),
        grid=(rows // HALF,),
        out_shape=(wide, wide, jax.ShapeDtypeStruct((1, rows), jnp.float32)),
        in_specs=[smem, smem, smem, block, block, whole, whole, block, block, lanes, block, block, column, column],
        out_specs=(block, block, pl.BlockSpec((1, HALF), lambda i: (0, i))),
        scratch_shapes=[pltpu.VMEM((rows, width), jnp.bfloat16)] * 2,
        name="last_tile",
        **params(rows, width),
    )(steps, sharp, shift, pic, cap, ahead, behind, *sums, *rest)


def pick(place, choices):
    picked = choices[0]
    for k in range(1, len(choices)):
        picked = jnp.where(place == k, choices[k], picked)
    return picked


def shards(picture_raw_features, caption_raw_features, peer_assignment, sharpness_factor, offset_term):
    size = peer_assignment.shape[1]
    rows = picture_raw_features.shape[0]
    steps, pic, cap, ahead, behind, pic_factor, cap_factor = start(
        peer_assignment, picture_raw_features, caption_raw_features
    )
    scalars = sharpness_factor, offset_term
    held = [cap, pic]
    for step in range(3):
        fields = [steps[FIELDS * step + k] for k in range(FIELDS)]
        if step == 0:
            compute, operands = own_tile, (*scalars, pic, cap)
        else:
            compute = functools.partial(cross_tile, step - 1)
            operands = steps, *scalars, pic, cap, ahead, behind, *sums
            ahead, behind = pick(fields[0], held), pick(fields[1], held)
        ahead, behind, *sums = step_branches(fields[2:5], size, compute, (ahead, behind, *operands))
        held += [ahead, behind]
    image_embedding_gradient, grad_text, row_loss = last_tile(
        4 * rows, 2, steps, *scalars, pic, cap, ahead, behind, sums,
        picture_raw_features, caption_raw_features, pic_factor, cap_factor,
    )
    return image_embedding_gradient, grad_text, row_loss.reshape(rows)


def solution(mesh):
    placed = (P(AXES, None), P(AXES, None), P(), P(), P())
    return jax.shard_map(
        shards,
        mesh=mesh,
        in_specs=placed,
        out_specs=(P(AXES, None), P(AXES, None), P(AXES)),
        check_vma=False,
    )
```

```python
import functools
import itertools

import jax
import jax.numpy as jnp
import numpy as np
from jax import lax
from jax.experimental import pallas as pl
from jax.experimental.pallas import tpu as pltpu
from jax.sharding import PartitionSpec as P

AXES = ("gx", "gy")
HALF = 256
LANES = 128
FIELDS = 4
ROWS_OF_PLAN = 8
ROUNDS = 3

DISTANCES = (
    1, 3, 4, 5, 9, 11, 12, 13, 15, 17, 19, 20, 21, 23, 24, 25, 27, 28, 29, 31, 32, 33, 35, 36, 37, 39, 41, 47, 55,
    59, 61, 63,
)
STEP_COST = (
    35, 38, 42, 53, 54, 58, 55, 48, 43, 40, 43, 58, 54, 66, 69, 59, 56, 48, 42, 36, 39, 49, 59, 61, 65, 63, 65, 68,
    64, 67, 65, 64,
)
STEP_OVERHEAD = 8


def route_tables(size):
    direct = np.full(size, 10**6)
    direct[0] = 0
    for distance, cost in zip(DISTANCES, STEP_COST):
        direct[distance] = direct[-distance % size] = cost + STEP_OVERHEAD
    cost, first = direct.copy(), np.arange(size)
    for step in range(1, size):
        by_two = direct[step] + np.roll(direct, step)
        first = np.where(by_two < cost, step, first)
        cost = np.minimum(cost, by_two)
    assert cost.max() < 10**6
    branch = np.zeros(size // 2 + 1, np.int32)
    branch[list(DISTANCES)] = np.arange(len(DISTANCES))
    return cost.astype(np.int32), first.astype(np.int32), branch


def plan(peers, cost, first, branch, out):
    size = peers.shape[1]
    node = [peers[r, 0] for r in range(ROUNDS)]

    def wrapped(gap):
        return jnp.where(gap < 0, gap + size, gap)

    best = None
    for order in itertools.permutations(range(ROUNDS)):
        total, fields = None, []
        for place, r in enumerate(order):
            gap, onward = node[r], jnp.int32(0)
            if place:
                other = wrapped(node[r] - node[order[place - 1]])
                onward = jnp.where(cost[other] < cost[gap], 1, 0)
                gap = jnp.where(onward == 1, other, gap)
            total = cost[gap] if total is None else total + cost[gap]
            fields += [gap, onward]
        if best is None:
            best, kept = total, fields
        else:
            better = total < best
            best = jnp.where(better, total, best)
            kept = [jnp.where(better, n, o) for n, o in zip(fields, kept)]

    def emit(row, onward, gap, wanted):
        out[FIELDS * row] = onward
        out[FIELDS * row + 1] = jnp.where(gap > size // 2, 1, 0)
        out[FIELDS * row + 2] = branch[jnp.minimum(gap, size - gap)]
        out[FIELDS * row + 3] = wanted

    row = jnp.int32(0)
    for r in range(ROUNDS):
        gap, onward = kept[2 * r], kept[2 * r + 1]
        step = first[gap]
        double = jnp.where(step == gap, 0, 1)
        emit(row, onward, step, 1 - double)
        emit(row + double, jnp.where(double == 1, 1, onward), wrapped(gap - step + step * (1 - double)), 1)
        row = row + 1 + double
    emit(row, jnp.int32(0), jnp.int32(1), jnp.int32(0))
    out[FIELDS * ROWS_OF_PLAN] = row


def start_kernel(
    peers, cost, first, branch, raw_pic, raw_cap,
    steps, pic, cap, ahead, behind, pic_factor, cap_factor, pic_grad, cap_grad, loss,
):
    @pl.when(pl.program_id(0) == 0)
    def _():
        plan(peers, cost, first, branch, steps)

    units = []
    for raw, unit, factor in ((raw_pic, pic, pic_factor), (raw_cap, cap, cap_factor)):
        wide = raw[...].astype(jnp.float32)
        scale = lax.rsqrt(jnp.sum(wide * wide, axis=-1, keepdims=True) + 1e-06)
        units.append((wide * scale).astype(jnp.bfloat16))
        unit[...] = units[-1]
        factor[...] = scale
    swap = steps[1]
    ahead[...] = jnp.where(swap == 1, units[0], units[1])
    behind[...] = jnp.where(swap == 1, units[1], units[0])


def start(peers, pic, cap):
    rows, width = pic.shape
    smem, block, whole, lanes, column = specs(rows, width)
    somewhere = pl.BlockSpec(memory_space=pl.ANY)
    unit = jax.ShapeDtypeStruct((rows, width), jnp.bfloat16)
    factor = jax.ShapeDtypeStruct((rows, 1), jnp.float32)
    wide = jax.ShapeDtypeStruct((rows, width), jnp.float32)
    fields = jax.ShapeDtypeStruct((FIELDS * ROWS_OF_PLAN + 1,), jnp.int32)
    return pl.pallas_call(
        start_kernel,
        grid=(rows // HALF,),
        out_shape=(
            fields, unit, unit, unit, unit, factor, factor, wide, wide, jax.ShapeDtypeStruct((rows, LANES), jnp.float32)
        ),
        in_specs=[smem, smem, smem, smem, block, block],
        out_specs=(smem, block, block, block, block, column, column, somewhere, somewhere, somewhere),
        name="start",
    )(peers, *map(jnp.asarray, route_tables(peers.shape[1])), pic, cap)


def shifted(x, by, size):
    return lax.ppermute(x, AXES, [(i, (i + by) % size) for i in range(size)])


def move(branch, ahead, behind, size):
    def mover(by):
        return lambda a, b: (shifted(a, -by, size), shifted(b, by, size))

    return lax.switch(branch, [mover(by) for by in DISTANCES], ahead, behind)


def scores(left, right, sharp, shift):
    dots = lax.dot_general(left, right, (((1,), (1,)), ((), ())), preferred_element_type=jnp.float32)
    return sharp * dots + shift


def odds_ratio(odds):
    total = 1.0 + odds
    guess = pl.reciprocal(total, approx=True)
    return odds * (guess * (2.0 - total * guess))


def log_total(odds):
    return jnp.where(odds < 1e-3, odds - 0.5 * odds * odds, jnp.log(1.0 + odds))


def folded(wide):
    return sum(wide[:, k : k + LANES] for k in range(0, wide.shape[1], LANES))


def product(coeff, entries):
    return lax.dot_general(coeff, entries, (((1,), (0,)), ((), ())), preferred_element_type=jnp.float32)


def side(left, right, sharp, shift):
    logits = scores(left, right, sharp, shift)
    odds = jnp.exp(logits)
    coeff = (sharp * odds_ratio(odds)).astype(jnp.bfloat16)
    return odds, product(coeff, right).astype(jnp.bfloat16).astype(jnp.float32)


def step_kernel(
    step, steps, sharp, shift, pic, cap, ahead, behind, pic_sum, cap_sum, loss_sum,
    pic_grad, cap_grad, loss, next_ahead, next_behind, peer_pic, peer_cap,
):
    here = FIELDS * step[0]
    swap, wanted = steps[here + 1], steps[here + 3]
    onward, next_swap = steps[here + 4], steps[here + 5]
    half = pl.ds(pl.multiple_of(pl.program_id(0) * HALF, HALF), HALF)

    @pl.when(pl.program_id(0) == 0)
    def _():
        peer_cap[...] = jnp.where(swap == 1, behind[...], ahead[...])
        peer_pic[...] = jnp.where(swap == 1, ahead[...], behind[...])

    next_cap = jnp.where(onward == 1, peer_cap[half, :], cap[...])
    next_pic = jnp.where(onward == 1, peer_pic[half, :], pic[...])
    next_ahead[...] = jnp.where(next_swap == 1, next_pic, next_cap)
    next_behind[...] = jnp.where(next_swap == 1, next_cap, next_pic)
    fresh = step[0] == 0
    pairs = ((pic_sum, pic_grad), (cap_sum, cap_grad), (loss_sum, loss))

    @pl.when(wanted == 1)
    def _():
        odds, part = side(pic[...], peer_cap[...], sharp[0], shift[0])
        pic_grad[...] = jnp.where(fresh, 0.0, pic_sum[...]) + part
        loss[...] = jnp.where(fresh, 0.0, loss_sum[...]) + folded(log_total(odds))
        odds, part = side(cap[...], peer_pic[...], sharp[0], shift[0])
        cap_grad[...] = jnp.where(fresh, 0.0, cap_sum[...]) + part

    @pl.when(wanted == 0)
    def _():
        for held, out in pairs:
            out[...] = jnp.where(fresh, 0.0, held[...])


def restored(raw, factor, grad):
    wide = raw[...].astype(jnp.float32)
    scale = factor[...]
    inner = jnp.sum(wide * grad, axis=-1, keepdims=True)
    return scale * grad - wide * (scale * scale * scale * inner)


def last_kernel(
    mean_of, sharp, shift, pic, cap, all_pic, all_cap, pic_sum, cap_sum, loss_sum,
    raw_pic, raw_cap, pic_factor, cap_factor, pic_grad, cap_grad, loss,
):
    columns = all_pic.shape[0]
    rows_at = lax.broadcasted_iota(jnp.int32, (HALF, columns), 0) + pl.program_id(0) * HALF
    columns_at = lax.broadcasted_iota(jnp.int32, (HALF, columns), 1)
    label = jnp.where(rows_at == columns_at, 1.0, 0.0)
    for left, right, held, raw, factor, grad in (
        (pic, all_cap, pic_sum, raw_pic, pic_factor, pic_grad),
        (cap, all_pic, cap_sum, raw_cap, cap_factor, cap_grad),
    ):
        logits = scores(left[...], right[...], sharp[0], shift[0])
        odds = jnp.exp(logits)
        if left is pic:
            own_loss = folded(log_total(odds) - label * logits)
        coeff = (sharp[0] * (odds_ratio(odds) - label)).astype(jnp.bfloat16)
        grad[...] = restored(raw, factor, held[...] + product(coeff, right[...]))
    ones = jnp.full((8, LANES), 1.0, jnp.float32)
    total = lax.dot_general(
        ones, loss_sum[...] + own_loss, (((1,), (1,)), ((), ())),
        precision=lax.Precision.HIGHEST, preferred_element_type=jnp.float32,
    )
    loss[...] = total[0:1, :] * (1.0 / mean_of)


def specs(rows, width):
    smem = pl.BlockSpec(memory_space=pltpu.SMEM)
    block = pl.BlockSpec((HALF, width), lambda i: (i, 0))
    whole = pl.BlockSpec((rows, width), lambda i: (0, 0))
    lanes = pl.BlockSpec((HALF, LANES), lambda i: (i, 0))
    column = pl.BlockSpec((HALF, 1), lambda i: (i, 0))
    return smem, block, whole, lanes, column


def params(rows, width):
    return dict(
        compiler_params=pltpu.CompilerParams(vmem_limit_bytes=40 * 2**20),
        cost_estimate=pl.CostEstimate(
            flops=8 * rows * rows * width, bytes_accessed=20 * rows * width, transcendentals=4 * rows * rows
        ),
    )


def step_tile(step, steps, sharp, shift, pic, cap, ahead, behind, *sums):
    rows, width = pic.shape
    smem, block, whole, lanes, column = specs(rows, width)
    wide = jax.ShapeDtypeStruct((rows, width), jnp.float32)
    unit = jax.ShapeDtypeStruct((rows, width), jnp.bfloat16)
    return pl.pallas_call(
        step_kernel,
        grid=(rows // HALF,),
        out_shape=(wide, wide, jax.ShapeDtypeStruct((rows, LANES), jnp.float32), unit, unit),
        in_specs=[smem, smem, smem, smem, block, block, whole, whole, block, block, lanes],
        out_specs=(block, block, lanes, block, block),
        scratch_shapes=[pltpu.VMEM((rows, width), jnp.bfloat16)] * 2,
        input_output_aliases={8: 0, 9: 1, 10: 2},
        name="step_tile",
        **params(rows, width),
    )(step, steps, sharp, shift, pic, cap, ahead, behind, *sums)


def last_tile(mean_of, sharp, shift, pic, cap, sums, *rest):
    rows, width = pic.shape
    smem, block, whole, lanes, column = specs(rows, width)
    wide = jax.ShapeDtypeStruct((rows, width), jnp.float32)
    return pl.pallas_call(
        functools.partial(last_kernel, mean_of),
        grid=(rows // HALF,),
        out_shape=(wide, wide, jax.ShapeDtypeStruct((1, rows), jnp.float32)),
        in_specs=[smem, smem, block, block, whole, whole, block, block, lanes, block, block, column, column],
        out_specs=(block, block, pl.BlockSpec((1, HALF), lambda i: (0, i))),
        name="last_tile",
        **params(rows, width),
    )(sharp, shift, pic, cap, pic, cap, *sums, *rest)


def shards(picture_raw_features, caption_raw_features, peer_assignment, sharpness_factor, offset_term):
    size = peer_assignment.shape[1]
    rows = picture_raw_features.shape[0]
    steps, pic, cap, ahead, behind, pic_factor, cap_factor, *sums = start(
        peer_assignment, picture_raw_features, caption_raw_features
    )
    scalars = sharpness_factor, offset_term

    def one_step(step, carry):
        ahead, behind, *sums = carry
        branch = lax.dynamic_index_in_dim(steps, FIELDS * step + 2, keepdims=False)
        ahead, behind = move(branch, ahead, behind, size)
        *sums, ahead, behind = step_tile(step.reshape(1), steps, *scalars, pic, cap, ahead, behind, *sums)
        return ahead, behind, *sums

    _, _, *sums = lax.fori_loop(0, steps[FIELDS * ROWS_OF_PLAN], one_step, (ahead, behind, *sums))
    image_embedding_gradient, grad_text, row_loss = last_tile(
        (ROUNDS + 1) * rows, *scalars, pic, cap, sums, picture_raw_features, caption_raw_features, pic_factor, cap_factor
    )
    return image_embedding_gradient, grad_text, row_loss.reshape(rows)


def solution(mesh):
    placed = (P(AXES, None), P(AXES, None), P(), P(), P())
    return jax.shard_map(
        shards,
        mesh=mesh,
        in_specs=placed,
        out_specs=(P(AXES, None), P(AXES, None), P(AXES)),
        check_vma=False,
    )
```

```python
import functools
import itertools

import jax
import jax.numpy as jnp
import numpy as np
from jax import lax
from jax.experimental import pallas as pl
from jax.experimental.pallas import tpu as pltpu
from jax.sharding import PartitionSpec as P

AXES = ("gx", "gy")
HALF = 256
LANES = 128
FIELDS = 4
ROWS_OF_PLAN = 8
ROUNDS = 3

DISTANCES = (
    1, 3, 4, 5, 9, 11, 12, 13, 15, 17, 19, 20, 21, 23, 24, 25, 27, 28, 29, 31, 32, 33, 35, 36, 37, 39, 41, 47, 55,
    59, 61, 63,
)
STEP_COST = (
    35, 38, 42, 53, 54, 58, 55, 48, 43, 40, 43, 58, 54, 66, 69, 59, 56, 48, 42, 36, 39, 49, 59, 61, 65, 63, 65, 68,
    64, 67, 65, 64,
)
STEP_OVERHEAD = 8


def route_tables(size):
    direct = np.full(size, 10**6)
    direct[0] = 0
    for distance, cost in zip(DISTANCES, STEP_COST):
        direct[distance] = direct[-distance % size] = cost + STEP_OVERHEAD
    cost, first = direct.copy(), np.arange(size)
    for step in range(1, size):
        by_two = direct[step] + np.roll(direct, step)
        first = np.where(by_two < cost, step, first)
        cost = np.minimum(cost, by_two)
    assert cost.max() < 10**6
    branch = np.zeros(size // 2 + 1, np.int32)
    branch[list(DISTANCES)] = np.arange(len(DISTANCES))
    return cost.astype(np.int32), first.astype(np.int32), branch


def plan(peers, cost, first, branch, out):
    size = peers.shape[1]
    node = [peers[r, 0] for r in range(ROUNDS)]

    def wrapped(gap):
        return jnp.where(gap < 0, gap + size, gap)

    best = None
    for order in itertools.permutations(range(ROUNDS)):
        total, fields = None, []
        for place, r in enumerate(order):
            gap, onward = node[r], jnp.int32(0)
            if place:
                other = wrapped(node[r] - node[order[place - 1]])
                onward = jnp.where(cost[other] < cost[gap], 1, 0)
                gap = jnp.where(onward == 1, other, gap)
            total = cost[gap] if total is None else total + cost[gap]
            fields += [gap, onward]
        if best is None:
            best, kept = total, fields
        else:
            better = total < best
            best = jnp.where(better, total, best)
            kept = [jnp.where(better, n, o) for n, o in zip(fields, kept)]

    def emit(row, onward, gap, partner):
        out[FIELDS * row] = onward
        out[FIELDS * row + 1] = jnp.where(gap > size // 2, 1, 0)
        out[FIELDS * row + 2] = branch[jnp.minimum(gap, size - gap)]
        out[FIELDS * row + 3] = partner

    row = jnp.int32(0)
    for r in range(ROUNDS):
        gap, onward = kept[2 * r], kept[2 * r + 1]
        step = first[gap]
        double = jnp.where(step == gap, 0, 1)
        emit(row, onward, step, jnp.where(double == 1, ROUNDS, r))
        emit(row + double, jnp.where(double == 1, 1, onward), wrapped(gap - step + step * (1 - double)), r)
        row = row + 1 + double
    emit(row, jnp.int32(0), jnp.int32(1), jnp.int32(ROUNDS))
    out[FIELDS * ROWS_OF_PLAN] = row


def start_kernel(
    peers, cost, first, branch, raw_pic, raw_cap,
    steps, first_branch, pic, cap, ahead, behind, pic_factor, cap_factor, pic_parts, cap_parts, losses,
    raw, unit, arrived, sent,
):
    loads = [pltpu.make_async_copy(src, raw.at[k], arrived.at[k]) for k, src in enumerate((raw_cap, raw_pic))]
    for load in loads:
        load.start()
    plan(peers, cost, first, branch, steps)
    first_branch[0] = steps[2]
    swap = steps[1]
    stores = []
    for k, (out, factor) in enumerate(((cap, cap_factor), (pic, pic_factor))):
        loads[k].wait()
        wide = raw[k].astype(jnp.float32)
        scale = lax.rsqrt(jnp.sum(wide * wide, axis=-1, keepdims=True) + 1e-06)
        unit[k] = (wide * scale).astype(jnp.bfloat16)
        factor[...] = scale
        stores.append(pltpu.make_async_copy(unit.at[k], out, sent.at[k]))
        stores[-1].start()
    for k, (out, place) in enumerate(((ahead, swap), (behind, 1 - swap))):
        stores.append(pltpu.make_async_copy(unit.at[place], out, sent.at[2 + k]))
        stores[-1].start()
    for store in stores:
        store.wait()


def start(peers, pic, cap):
    rows, width = pic.shape
    smem = pl.BlockSpec(memory_space=pltpu.SMEM)
    vmem = pl.BlockSpec(memory_space=pltpu.VMEM)
    somewhere = pl.BlockSpec(memory_space=pl.ANY)
    unit = jax.ShapeDtypeStruct((rows, width), jnp.bfloat16)
    factor = jax.ShapeDtypeStruct((rows, 1), jnp.float32)
    parts = jax.ShapeDtypeStruct((ROUNDS, rows, width), jnp.bfloat16)
    fields = jax.ShapeDtypeStruct((FIELDS * ROWS_OF_PLAN + 1,), jnp.int32)
    return pl.pallas_call(
        start_kernel,
        out_shape=(
            fields, jax.ShapeDtypeStruct((1,), jnp.int32), unit, unit, unit, unit, factor, factor, parts, parts,
            jax.ShapeDtypeStruct((ROUNDS, rows, LANES), jnp.float32),
        ),
        in_specs=[smem] * 4 + [somewhere] * 2,
        out_specs=(smem, smem, *[somewhere] * 4, vmem, vmem, *[somewhere] * 3),
        scratch_shapes=[
            pltpu.VMEM((2, rows, width), jnp.bfloat16),
            pltpu.VMEM((2, rows, width), jnp.bfloat16),
            pltpu.SemaphoreType.DMA((2,)),
            pltpu.SemaphoreType.DMA((4,)),
        ],
        compiler_params=pltpu.CompilerParams(vmem_limit_bytes=40 * 2**20),
        name="start",
    )(peers, *map(jnp.asarray, route_tables(peers.shape[1])), pic, cap)


def shifted(x, by, size):
    return lax.ppermute(x, AXES, [(i, (i + by) % size) for i in range(size)])


def move(branch, ahead, behind, size):
    def mover(by):
        return lambda a, b: (shifted(a, -by, size), shifted(b, by, size))

    return lax.switch(branch, [mover(by) for by in DISTANCES], ahead, behind)


def scores(left, right, sharp, shift):
    dots = lax.dot_general(left, right, (((1,), (1,)), ((), ())), preferred_element_type=jnp.float32)
    return sharp * dots + shift


def odds_ratio(odds):
    total = 1.0 + odds
    guess = pl.reciprocal(total, approx=True)
    return odds * (guess * (2.0 - total * guess))


def log_total(odds):
    return jnp.where(odds < 1e-3, odds - 0.5 * odds * odds, jnp.log(1.0 + odds))


def folded(wide):
    return sum(wide[:, k : k + LANES] for k in range(0, wide.shape[1], LANES))


def product(coeff, entries):
    return lax.dot_general(coeff, entries, (((1,), (0,)), ((), ())), preferred_element_type=jnp.float32)


def step_kernel(
    step, steps, sharp, shift, pic, cap, ahead, behind, old_pic_parts, old_cap_parts, old_losses,
    pic_parts, cap_parts, losses, next_ahead, next_behind, next_branch,
    held, part, loss, arrived, sent, kept,
):
    here = FIELDS * step[0]
    swap, partner = steps[here + 1], steps[here + 3]
    onward, next_swap = steps[here + 4], steps[here + 5]
    next_branch[0] = steps[here + 6]
    loads = [
        pltpu.make_async_copy(src, held.at[place], arrived.at[k])
        for k, (src, place) in enumerate(((ahead, 2 + swap), (behind, 3 - swap), (pic, 1), (cap, 0)))
    ]
    for load in loads:
        load.start()
    for load in loads:
        load.wait()
    stores = [
        pltpu.make_async_copy(held.at[2 * onward + place], out, sent.at[k])
        for k, (out, place) in enumerate(((next_ahead, next_swap), (next_behind, 1 - next_swap)))
    ]
    for store in stores:
        store.start()

    @pl.when(partner < ROUNDS)
    def _():
        keeps = []
        for k, (left, right, out) in enumerate(((1, 2, pic_parts), (0, 3, cap_parts))):
            for first in range(0, held.shape[1], HALF):
                rows = slice(first, first + HALF)
                odds = jnp.exp(scores(held[left, rows, :], held[right], sharp[0], shift[0]))
                coeff = (sharp[0] * odds_ratio(odds)).astype(jnp.bfloat16)
                if k == 0:
                    loss[rows, :] = folded(log_total(odds))
                part[k, rows, :] = product(coeff, held[right]).astype(jnp.bfloat16)
                keeps.append(
                    pltpu.make_async_copy(part.at[k, rows], out.at[partner, rows], kept.at[len(keeps)])
                )
                keeps[-1].start()
        keeps.append(pltpu.make_async_copy(loss, losses.at[partner], kept.at[len(keeps)]))
        keeps[-1].start()
        for keep in keeps:
            keep.wait()

    for store in stores:
        store.wait()


def restored(raw, factor, grad):
    wide = raw[...].astype(jnp.float32)
    scale = factor[...]
    inner = jnp.sum(wide * grad, axis=-1, keepdims=True)
    return scale * grad - wide * (scale * scale * scale * inner)


def last_kernel(
    mean_of, sharp, shift, pic, cap, all_pic, all_cap, pic_parts, cap_parts, losses,
    raw_pic, raw_cap, pic_factor, cap_factor, pic_grad, cap_grad, loss,
):
    columns = all_pic.shape[0]
    rows_at = lax.broadcasted_iota(jnp.int32, (HALF, columns), 0) + pl.program_id(0) * HALF
    columns_at = lax.broadcasted_iota(jnp.int32, (HALF, columns), 1)
    label = jnp.where(rows_at == columns_at, 1.0, 0.0)
    for left, right, held, raw, factor, grad in (
        (pic, all_cap, pic_parts, raw_pic, pic_factor, pic_grad),
        (cap, all_pic, cap_parts, raw_cap, cap_factor, cap_grad),
    ):
        logits = scores(left[...], right[...], sharp[0], shift[0])
        odds = jnp.exp(logits)
        if left is pic:
            own_loss = folded(log_total(odds) - label * logits)
        coeff = (sharp[0] * (odds_ratio(odds) - label)).astype(jnp.bfloat16)
        parts = sum(held[r].astype(jnp.float32) for r in range(ROUNDS))
        grad[...] = restored(raw, factor, product(coeff, right[...]) + parts)
    ones = jnp.full((8, LANES), 1.0, jnp.float32)
    total = lax.dot_general(
        ones, own_loss + sum(losses[r] for r in range(ROUNDS)), (((1,), (1,)), ((), ())),
        precision=lax.Precision.HIGHEST, preferred_element_type=jnp.float32,
    )
    loss[...] = total[0:1, :] * (1.0 / mean_of)


def specs(rows, width):
    smem = pl.BlockSpec(memory_space=pltpu.SMEM)
    block = pl.BlockSpec((HALF, width), lambda i: (i, 0))
    whole = pl.BlockSpec((rows, width), lambda i: (0, 0))
    column = pl.BlockSpec((HALF, 1), lambda i: (i, 0))
    return smem, block, whole, column


def params(rows, width):
    return dict(
        compiler_params=pltpu.CompilerParams(vmem_limit_bytes=40 * 2**20),
        cost_estimate=pl.CostEstimate(
            flops=8 * rows * rows * width, bytes_accessed=20 * rows * width, transcendentals=4 * rows * rows
        ),
    )


def step_tile(step, steps, sharp, shift, pic, cap, ahead, behind, *parts):
    rows, width = pic.shape
    smem = pl.BlockSpec(memory_space=pltpu.SMEM)
    somewhere = pl.BlockSpec(memory_space=pl.ANY)
    unit = jax.ShapeDtypeStruct((rows, width), jnp.bfloat16)
    return pl.pallas_call(
        step_kernel,
        out_shape=(
            *[jax.ShapeDtypeStruct(p.shape, p.dtype) for p in parts], unit, unit, jax.ShapeDtypeStruct((1,), jnp.int32)
        ),
        in_specs=[smem] * 4 + [somewhere] * 7,
        out_specs=(*[somewhere] * 5, smem),
        scratch_shapes=[
            pltpu.VMEM((4, rows, width), jnp.bfloat16),
            pltpu.VMEM((2, rows, width), jnp.bfloat16),
            pltpu.VMEM((rows, LANES), jnp.float32),
            pltpu.SemaphoreType.DMA((4,)),
            pltpu.SemaphoreType.DMA((2,)),
            pltpu.SemaphoreType.DMA((2 * rows // HALF + 1,)),
        ],
        input_output_aliases={8: 0, 9: 1, 10: 2},
        name="step_tile",
        **params(rows, width),
    )(step, steps, sharp, shift, pic, cap, ahead, behind, *parts)


def last_tile(mean_of, sharp, shift, pic, cap, parts, *rest):
    rows, width = pic.shape
    smem, block, whole, column = specs(rows, width)
    wide = jax.ShapeDtypeStruct((rows, width), jnp.float32)
    several = pl.BlockSpec((ROUNDS, HALF, width), lambda i: (0, i, 0))
    return pl.pallas_call(
        functools.partial(last_kernel, mean_of),
        grid=(rows // HALF,),
        out_shape=(wide, wide, jax.ShapeDtypeStruct((1, rows), jnp.float32)),
        in_specs=[
            smem, smem, block, block, whole, whole, several, several,
            pl.BlockSpec((ROUNDS, HALF, LANES), lambda i: (0, i, 0)), block, block, column, column,
        ],
        out_specs=(block, block, pl.BlockSpec((1, HALF), lambda i: (0, i))),
        name="last_tile",
        **params(rows, width),
    )(sharp, shift, pic, cap, pic, cap, *parts, *rest)


def shards(picture_raw_features, caption_raw_features, peer_assignment, sharpness_factor, offset_term):
    size = peer_assignment.shape[1]
    rows = picture_raw_features.shape[0]
    steps, branch, pic, cap, ahead, behind, pic_factor, cap_factor, *parts = start(
        peer_assignment, picture_raw_features, caption_raw_features
    )
    scalars = sharpness_factor, offset_term

    def one_step(step, carry):
        branch, ahead, behind, *parts = carry
        ahead, behind = move(branch[0], ahead, behind, size)
        *parts, ahead, behind, branch = step_tile(step.reshape(1), steps, *scalars, pic, cap, ahead, behind, *parts)
        return branch, ahead, behind, *parts

    _, _, _, *parts = lax.fori_loop(0, steps[FIELDS * ROWS_OF_PLAN], one_step, (branch, ahead, behind, *parts))
    image_embedding_gradient, grad_text, row_loss = last_tile(
        (ROUNDS + 1) * rows, *scalars, pic, cap, parts, picture_raw_features, caption_raw_features, pic_factor, cap_factor
    )
    return image_embedding_gradient, grad_text, row_loss.reshape(rows)


def solution(mesh):
    placed = (P(AXES, None), P(AXES, None), P(), P(), P())
    return jax.shard_map(
        shards,
        mesh=mesh,
        in_specs=placed,
        out_specs=(P(AXES, None), P(AXES, None), P(AXES)),
        check_vma=False,
    )
```

```python
import functools
import itertools

import jax
import jax.numpy as jnp
import numpy as np
from jax import lax
from jax.experimental import pallas as pl
from jax.experimental.pallas import tpu as pltpu
from jax.sharding import PartitionSpec as P

AXES = ("gx", "gy")
HALF = 256
LANES = 128
FIELDS = 4
ROWS_OF_PLAN = 8
ROUNDS = 3
VMEM_LIMIT = 60 * 2**20

DISTANCES = (
    1, 3, 4, 5, 7, 9, 12, 13, 14, 15, 16, 17, 18, 19, 20, 21, 25, 27, 28, 29, 31, 32, 33, 34, 35, 36, 37, 43, 55,
    56, 60, 61,
)
STEP_COST = (
    40, 45, 42, 53, 63, 54, 61, 50, 60, 42, 59, 45, 63, 46, 56, 53, 58, 54, 48, 47, 39, 41, 44, 64, 52, 56, 67, 65,
    58, 66, 65, 60,
)
STEP_OVERHEAD = 6


def route_tables(size):
    direct = np.full(size, 10**6)
    direct[0] = 0
    for distance, cost in zip(DISTANCES, STEP_COST):
        direct[distance] = direct[-distance % size] = cost + STEP_OVERHEAD
    cost, first = direct.copy(), np.arange(size)
    for step in range(1, size):
        by_two = direct[step] + np.roll(direct, step)
        first = np.where(by_two < cost, step, first)
        cost = np.minimum(cost, by_two)
    assert cost.max() < 10**6
    branch = np.zeros(size // 2 + 1, np.int32)
    branch[list(DISTANCES)] = np.arange(len(DISTANCES))
    table = np.zeros((3, size), np.int32)
    table[0], table[1], table[2, : branch.size] = cost, first, branch
    return table


def plan(peers, table, out):
    size = peers.shape[1]
    node = [peers[r, 0] for r in range(ROUNDS)]

    def wrapped(gap):
        return jnp.where(gap < 0, gap + size, gap)

    best = None
    for order in itertools.permutations(range(ROUNDS)):
        total, fields = None, []
        for place, r in enumerate(order):
            gap, onward = node[r], jnp.int32(0)
            if place:
                other = wrapped(node[r] - node[order[place - 1]])
                onward = jnp.where(table[0, other] < table[0, gap], 1, 0)
                gap = jnp.where(onward == 1, other, gap)
            total = table[0, gap] if total is None else total + table[0, gap]
            fields += [gap, onward]
        if best is None:
            best, kept = total, fields
        else:
            better = total < best
            best = jnp.where(better, total, best)
            kept = [jnp.where(better, n, o) for n, o in zip(fields, kept)]

    def emit(row, onward, gap, partner):
        out[FIELDS * row] = onward
        out[FIELDS * row + 1] = jnp.where(gap > size // 2, 1, 0)
        out[FIELDS * row + 2] = table[2, jnp.minimum(gap, size - gap)]
        out[FIELDS * row + 3] = partner

    row = jnp.int32(0)
    for r in range(ROUNDS):
        gap, onward = kept[2 * r], kept[2 * r + 1]
        step = table[1, gap]
        double = jnp.where(step == gap, 0, 1)
        emit(row, onward, step, jnp.where(double == 1, ROUNDS, r))
        emit(row + double, jnp.where(double == 1, 1, onward), wrapped(gap - step + step * (1 - double)), r)
        row = row + 1 + double
    emit(row, jnp.int32(0), jnp.int32(1), jnp.int32(ROUNDS))
    out[FIELDS * ROWS_OF_PLAN] = row


def start_kernel(
    peers, table, raw_pic, raw_cap, steps, first_branch, blocks, ahead, behind, pic_factor, cap_factor,
    raw, unit, arrived, sent,
):
    loads = [pltpu.make_async_copy(src, raw.at[k], arrived.at[k]) for k, src in enumerate((raw_cap, raw_pic))]
    for load in loads:
        load.start()
    plan(peers, table, steps)
    first_branch[0] = steps[2]
    swap = steps[1]
    for k, factor in enumerate((cap_factor, pic_factor)):
        loads[k].wait()
        wide = raw[k].astype(jnp.float32)
        scale = lax.rsqrt(jnp.sum(wide * wide, axis=-1, keepdims=True) + 1e-06)
        unit[k] = (wide * scale).astype(jnp.bfloat16)
        factor[...] = scale
    stores = [
        pltpu.make_async_copy(unit.at[place], out, sent.at[k])
        for k, (place, out) in enumerate(((swap, ahead), (1 - swap, behind), (0, blocks.at[0]), (1, blocks.at[1])))
    ]
    for store in stores:
        store.start()
    for store in stores:
        store.wait()


def start(peers, pic, cap):
    rows, width = pic.shape
    smem = pl.BlockSpec(memory_space=pltpu.SMEM)
    vmem = pl.BlockSpec(memory_space=pltpu.VMEM)
    somewhere = pl.BlockSpec(memory_space=pl.ANY)
    unit = jax.ShapeDtypeStruct((rows, width), jnp.bfloat16)
    factor = jax.ShapeDtypeStruct((rows, 1), jnp.float32)
    blocks = jax.ShapeDtypeStruct((2 * ROUNDS + 2, rows, width), jnp.bfloat16)
    fields = jax.ShapeDtypeStruct((FIELDS * ROWS_OF_PLAN + 1,), jnp.int32)
    return pl.pallas_call(
        start_kernel,
        out_shape=(fields, jax.ShapeDtypeStruct((1,), jnp.int32), blocks, unit, unit, factor, factor),
        in_specs=[smem, smem, somewhere, somewhere],
        out_specs=(smem, smem, somewhere, somewhere, somewhere, vmem, vmem),
        scratch_shapes=[
            pltpu.VMEM((2, rows, width), jnp.bfloat16),
            pltpu.VMEM((2, rows, width), jnp.bfloat16),
            pltpu.SemaphoreType.DMA((2,)),
            pltpu.SemaphoreType.DMA((4,)),
        ],
        compiler_params=pltpu.CompilerParams(vmem_limit_bytes=VMEM_LIMIT),
        name="start",
    )(peers, jnp.asarray(route_tables(peers.shape[1])), pic, cap)


def shifted(x, by, size):
    return lax.ppermute(x, AXES, [(i, (i + by) % size) for i in range(size)])


def move(branch, ahead, behind, size):
    def mover(by):
        return lambda a, b: (shifted(a, -by, size), shifted(b, by, size))

    return lax.switch(branch, [mover(by) for by in DISTANCES], ahead, behind)


def scores(left, right, sharp, shift):
    dots = lax.dot_general(left, right, (((1,), (1,)), ((), ())), preferred_element_type=jnp.float32)
    return sharp * dots + shift


def odds_ratio(odds):
    total = 1.0 + odds
    guess = pl.reciprocal(total, approx=True)
    return odds * (guess * (2.0 - total * guess))


def log_total(odds):
    return jnp.where(odds < 1e-3, odds - 0.5 * odds * odds, jnp.log(1.0 + odds))


def folded(wide):
    return sum(wide[:, k : k + LANES] for k in range(0, wide.shape[1], LANES))


def product(coeff, entries):
    return lax.dot_general(coeff, entries, (((1,), (0,)), ((), ())), preferred_element_type=jnp.float32)


def pass_kernel(
    step, steps, ahead, behind, old_blocks, blocks, next_ahead, next_behind, next_branch, kept, sent,
):
    here = FIELDS * step[0]
    swap, partner = steps[here + 1], steps[here + 3]
    onward, next_swap = steps[here + 4], steps[here + 5]
    next_branch[0] = steps[here + 6]
    wanted = partner < ROUNDS
    more = step[0] + 1 < steps[FIELDS * ROWS_OF_PLAN]
    crossed = swap != next_swap

    def copies(sources, outs, sems):
        return [pltpu.make_async_copy(src, out, sems.at[k]) for k, (src, out) in enumerate(zip(sources, outs))]

    def start_all(sources, outs, sems):
        for copy in copies(sources, outs, sems):
            copy.start()

    place = jnp.where(wanted, 2 + 2 * partner, 2)
    keeps = (ahead, behind), (blocks.at[place + swap], blocks.at[place + 1 - swap]), kept
    nexts = next_ahead, next_behind

    @pl.when(jnp.logical_and(more, jnp.logical_and(onward == 1, jnp.logical_not(crossed))))
    def _():
        start_all((ahead, behind), nexts, sent)

    @pl.when(jnp.logical_and(more, jnp.logical_and(onward == 1, crossed)))
    def _():
        start_all((behind, ahead), nexts, sent)

    @pl.when(jnp.logical_and(more, onward == 0))
    def _():
        start_all((blocks.at[next_swap], blocks.at[1 - next_swap]), nexts, sent)

    @pl.when(wanted)
    def _():
        start_all(*keeps)
        for copy in copies(*keeps):
            copy.wait()

    @pl.when(more)
    def _():
        for copy in copies((ahead, behind), nexts, sent):
            copy.wait()


def tiles_kernel(
    mean_of, sharp, shift, blocks, raw_cap, raw_pic, cap_factor, pic_factor, cap_grad, pic_grad, loss,
    held, raw, sums, losses, arrived, sent,
):
    slots, rows = held.shape[0] // 2, held.shape[1]
    sources = [blocks.at[k] for k in range(2 * slots)] + [raw_pic, raw_cap]
    places = [held.at[k] for k in range(2 * slots)] + [raw.at[0], raw.at[1]]
    loads = [pltpu.make_async_copy(src, out, arrived.at[k]) for k, (src, out) in enumerate(zip(sources, places))]
    for load in loads:
        load.start()
    rows_at = lax.broadcasted_iota(jnp.int32, (HALF, rows), 0)
    columns_at = lax.broadcasted_iota(jnp.int32, (HALF, rows), 1)

    @pl.loop(0, slots)
    def _(slot):
        own = slot == 0
        for k in range(2):
            pltpu.make_async_copy(blocks.at[2 * slot + k], held.at[2 * slot + k], arrived.at[2 * slot + k]).wait()

        @pl.loop(0, 2 * rows // HALF)
        def _(turn):
            side = turn % 2
            first = pl.multiple_of(turn // 2 * HALF, HALF)
            here = pl.ds(first, HALF)
            right = 2 * slot + side
            logits = scores(held[1 - side, here, :], held[right], sharp[0], shift[0])
            odds = jnp.exp(logits)
            label = jnp.where(jnp.logical_and(own, rows_at + first == columns_at), 1.0, 0.0)
            coeff = (sharp[0] * (odds_ratio(odds) - label)).astype(jnp.bfloat16)
            part = product(coeff, held[right])
            lost = folded(log_total(odds) - label * logits)

            @pl.when(own)
            def _():
                sums[side, here, :] = part
                losses[side, here, :] = lost

            @pl.when(jnp.logical_not(own))
            def _():
                sums[side, here, :] += part.astype(jnp.bfloat16).astype(jnp.float32)
                losses[side, here, :] += lost

    for load in loads[2 * slots :]:
        load.wait()
    stores = []
    for side, (factor, grad) in enumerate(((pic_factor, pic_grad), (cap_factor, cap_grad))):
        for first in range(0, rows, HALF):
            here = slice(first, first + HALF)
            wide = raw[side, here, :].astype(jnp.float32)
            scale = factor[here, :]
            total = sums[side, here, :]
            inner = jnp.sum(wide * total, axis=-1, keepdims=True)
            sums[side, here, :] = scale * total - wide * (scale * scale * scale * inner)
            stores.append(pltpu.make_async_copy(sums.at[side, here], grad.at[here], sent.at[len(stores)]))
            stores[-1].start()
    ones = jnp.full((8, LANES), 1.0, jnp.float32)
    total = lax.dot_general(
        ones, losses[0], (((1,), (1,)), ((), ())),
        precision=lax.Precision.HIGHEST, preferred_element_type=jnp.float32,
    )
    loss[...] = total[0:1, :] * (1.0 / mean_of)
    for store in stores:
        store.wait()


def pass_on(step, steps, ahead, behind, blocks):
    smem = pl.BlockSpec(memory_space=pltpu.SMEM)
    somewhere = pl.BlockSpec(memory_space=pl.ANY)
    unit = jax.ShapeDtypeStruct(ahead.shape, ahead.dtype)
    return pl.pallas_call(
        pass_kernel,
        out_shape=(
            jax.ShapeDtypeStruct(blocks.shape, blocks.dtype), unit, unit, jax.ShapeDtypeStruct((1,), jnp.int32)
        ),
        in_specs=[smem] * 2 + [somewhere] * 3,
        out_specs=(*[somewhere] * 3, smem),
        scratch_shapes=[pltpu.SemaphoreType.DMA((2,)), pltpu.SemaphoreType.DMA((2,))],
        input_output_aliases={4: 0},
        name="pass_on",
    )(step, steps, ahead, behind, blocks)


def all_tiles(mean_of, sharp, shift, blocks, raw_cap, raw_pic, cap_factor, pic_factor):
    count, rows, width = blocks.shape
    smem = pl.BlockSpec(memory_space=pltpu.SMEM)
    vmem = pl.BlockSpec(memory_space=pltpu.VMEM)
    somewhere = pl.BlockSpec(memory_space=pl.ANY)
    wide = jax.ShapeDtypeStruct((rows, width), jnp.float32)
    return pl.pallas_call(
        functools.partial(tiles_kernel, mean_of),
        out_shape=(wide, wide, jax.ShapeDtypeStruct((1, rows), jnp.float32)),
        in_specs=[smem, smem, somewhere, somewhere, somewhere, vmem, vmem],
        out_specs=(somewhere, somewhere, vmem),
        scratch_shapes=[
            pltpu.VMEM((count, rows, width), jnp.bfloat16),
            pltpu.VMEM((2, rows, width), jnp.bfloat16),
            pltpu.VMEM((2, rows, width), jnp.float32),
            pltpu.VMEM((2, rows, LANES), jnp.float32),
            pltpu.SemaphoreType.DMA((count + 2,)),
            pltpu.SemaphoreType.DMA((2 * rows // HALF,)),
        ],
        compiler_params=pltpu.CompilerParams(vmem_limit_bytes=VMEM_LIMIT),
        name="all_tiles",
    )(sharp, shift, blocks, raw_cap, raw_pic, cap_factor, pic_factor)


def shards(picture_raw_features, caption_raw_features, peer_assignment, sharpness_factor, offset_term):
    size = peer_assignment.shape[1]
    rows = picture_raw_features.shape[0]
    steps, branch, blocks, ahead, behind, pic_factor, cap_factor = start(
        peer_assignment, picture_raw_features, caption_raw_features
    )

    def one_step(step, carry):
        branch, ahead, behind, blocks = carry
        ahead, behind = move(branch[0], ahead, behind, size)
        blocks, ahead, behind, branch = pass_on(step.reshape(1), steps, ahead, behind, blocks)
        return branch, ahead, behind, blocks

    _, _, _, blocks = lax.fori_loop(0, steps[FIELDS * ROWS_OF_PLAN], one_step, (branch, ahead, behind, blocks))
    grad_text, image_embedding_gradient, row_loss = all_tiles(
        (ROUNDS + 1) * rows, sharpness_factor, offset_term, blocks,
        caption_raw_features, picture_raw_features, cap_factor, pic_factor,
    )
    return image_embedding_gradient, grad_text, row_loss.reshape(rows)


def solution(mesh):
    placed = (P(AXES, None), P(AXES, None), P(), P(), P())
    return jax.shard_map(
        shards,
        mesh=mesh,
        in_specs=placed,
        out_specs=(P(AXES, None), P(AXES, None), P(AXES)),
        check_vma=False,
    )
```

```python
import functools
import itertools

import jax
import jax.numpy as jnp
import numpy as np
from jax import lax
from jax.experimental import pallas as pl
from jax.experimental.pallas import tpu as pltpu
from jax.sharding import PartitionSpec as P

AXES = ("gx", "gy")
HALF = 256
LANES = 128
FIELDS = 4
ROWS_OF_PLAN = 8
ROUNDS = 3
VMEM_LIMIT = 32 * 2**20
START_VMEM_LIMIT = 55 * 2**20

DISTANCES = (
    2, 3, 5, 9, 10, 15, 16, 17, 19, 21, 27, 29, 31, 33, 35, 39, 55, 59, 61, 62, 1, 4, 12, 13, 20, 28, 32, 36,
)
STEP_COST = (
    58, 45, 53, 54, 65, 42, 59, 45, 46, 53, 54, 47, 39, 44, 52, 60, 58, 58, 60, 67, 35, 38, 49, 38, 52, 34, 28, 48,
)
STEP_OVERHEAD = 6


def route_tables(size):
    direct = np.full(size, 10**6)
    direct[0] = 0
    for distance, cost in zip(DISTANCES, STEP_COST):
        direct[distance] = direct[-distance % size] = cost + STEP_OVERHEAD
    cost, first = direct.copy(), np.arange(size)
    for step in range(1, size):
        by_two = direct[step] + np.roll(direct, step)
        first = np.where(by_two < cost, step, first)
        cost = np.minimum(cost, by_two)
    assert cost.max() < 10**6
    branch = np.zeros(size // 2 + 1, np.int32)
    branch[list(DISTANCES)] = np.arange(len(DISTANCES))
    table = np.zeros((3, size), np.int32)
    table[0], table[1], table[2, : branch.size] = cost, first, branch
    return table


def plan(peers, table, out):
    size = peers.shape[1]
    node = [peers[r, 0] for r in range(ROUNDS)]

    def wrapped(gap):
        return jnp.where(gap < 0, gap + size, gap)

    best = None
    for order in itertools.permutations(range(ROUNDS)):
        total, fields = None, []
        for place, r in enumerate(order):
            gap, onward = node[r], jnp.int32(0)
            if place:
                other = wrapped(node[r] - node[order[place - 1]])
                onward = jnp.where(table[0, other] < table[0, gap], 1, 0)
                gap = jnp.where(onward == 1, other, gap)
            total = table[0, gap] if total is None else total + table[0, gap]
            fields += [gap, onward]
        if best is None:
            best, kept = total, fields
        else:
            better = total < best
            best = jnp.where(better, total, best)
            kept = [jnp.where(better, n, o) for n, o in zip(fields, kept)]

    def emit(row, onward, gap, partner):
        out[FIELDS * row] = onward
        out[FIELDS * row + 1] = jnp.where(gap > size // 2, 1, 0)
        out[FIELDS * row + 2] = table[2, jnp.minimum(gap, size - gap)]
        out[FIELDS * row + 3] = partner

    row = jnp.int32(0)
    for r in range(ROUNDS):
        gap, onward = kept[2 * r], kept[2 * r + 1]
        step = table[1, gap]
        double = jnp.where(step == gap, 0, 1)
        emit(row, onward, step, jnp.where(double == 1, ROUNDS, r))
        emit(row + double, jnp.where(double == 1, 1, onward), wrapped(gap - step + step * (1 - double)), r)
        row = row + 1 + double
    emit(row, jnp.int32(0), jnp.int32(1), jnp.int32(ROUNDS))
    out[FIELDS * ROWS_OF_PLAN] = row


def start_kernel(
    peers, table, raw_pic, raw_cap,
    steps, first_branch, pic, cap, ahead, behind, pic_factor, cap_factor, pic_parts, cap_parts, losses,
    raw, arrived, sent,
):
    loads = [pltpu.make_async_copy(src, raw.at[k], arrived.at[k]) for k, src in enumerate((raw_cap, raw_pic))]
    for load in loads:
        load.start()
    plan(peers, table, steps)
    first_branch[0] = steps[2]
    swap = steps[1]
    for k, (unit, factor) in enumerate(((cap, cap_factor), (pic, pic_factor))):
        loads[k].wait()
        wide = raw[k].astype(jnp.float32)
        scale = lax.rsqrt(jnp.sum(wide * wide, axis=-1, keepdims=True) + 1e-06)
        unit[...] = (wide * scale).astype(jnp.bfloat16)
        factor[...] = scale
    lay_out(swap, cap, pic, ahead, behind, sent)
    wait_for_layout(cap, pic, ahead, behind, sent)


def lay_out(swap, texts, images, ahead, behind, sent):
    @pl.when(swap == 0)
    def _():
        pltpu.make_async_copy(texts, ahead, sent.at[0]).start()
        pltpu.make_async_copy(images, behind, sent.at[1]).start()

    @pl.when(swap != 0)
    def _():
        pltpu.make_async_copy(images, ahead, sent.at[0]).start()
        pltpu.make_async_copy(texts, behind, sent.at[1]).start()


def wait_for_layout(texts, images, ahead, behind, sent):
    pltpu.make_async_copy(texts, ahead, sent.at[0]).wait()
    pltpu.make_async_copy(images, behind, sent.at[1]).wait()


def start(peers, pic, cap):
    rows, width = pic.shape
    smem = pl.BlockSpec(memory_space=pltpu.SMEM)
    vmem = pl.BlockSpec(memory_space=pltpu.VMEM)
    somewhere = pl.BlockSpec(memory_space=pl.ANY)
    unit = jax.ShapeDtypeStruct((rows, width), jnp.bfloat16)
    factor = jax.ShapeDtypeStruct((rows, 1), jnp.float32)
    parts = jax.ShapeDtypeStruct((ROUNDS, rows, width), jnp.bfloat16)
    fields = jax.ShapeDtypeStruct((FIELDS * ROWS_OF_PLAN + 1,), jnp.int32)
    return pl.pallas_call(
        start_kernel,
        out_shape=(
            fields, jax.ShapeDtypeStruct((1,), jnp.int32), unit, unit, unit, unit, factor, factor, parts, parts,
            jax.ShapeDtypeStruct((ROUNDS, rows, LANES), jnp.float32),
        ),
        in_specs=[smem, smem, somewhere, somewhere],
        out_specs=(smem, smem, *[vmem] * 6, *[somewhere] * 3),
        scratch_shapes=[
            pltpu.VMEM((2, rows, width), jnp.bfloat16),
            pltpu.SemaphoreType.DMA((2,)),
            pltpu.SemaphoreType.DMA((2,)),
        ],
        compiler_params=pltpu.CompilerParams(vmem_limit_bytes=START_VMEM_LIMIT),
        name="start",
    )(peers, jnp.asarray(route_tables(peers.shape[1])), pic, cap)


def shifted(x, by, size):
    return lax.ppermute(x, AXES, [(i, (i + by) % size) for i in range(size)])


def move(branch, ahead, behind, size):
    def mover(by):
        return lambda a, b: (shifted(a, -by, size), shifted(b, by, size))

    return lax.switch(branch, [mover(by) for by in DISTANCES], ahead, behind)


def scores(left, right, sharp, shift):
    dots = lax.dot_general(left, right, (((1,), (1,)), ((), ())), preferred_element_type=jnp.float32)
    return sharp * dots + shift


def odds_ratio(odds):
    total = 1.0 + odds
    guess = pl.reciprocal(total, approx=True)
    return odds * (guess * (2.0 - total * guess))


def log_total(odds):
    return jnp.where(odds < 1e-3, odds - 0.5 * odds * odds, jnp.log(1.0 + odds))


def folded(wide):
    return sum(wide[:, k : k + LANES] for k in range(0, wide.shape[1], LANES))


def product(coeff, entries):
    return lax.dot_general(coeff, entries, (((1,), (0,)), ((), ())), preferred_element_type=jnp.float32)


def step_kernel(
    step, steps, sharp, shift, pic, cap, ahead, behind, old_pic_parts, old_cap_parts, old_losses,
    pic_parts, cap_parts, losses, next_ahead, next_behind, next_branch,
    peer, part, loss, arrived, sent, kept,
):
    here = FIELDS * step[0]
    swap, partner = steps[here + 1], steps[here + 3]
    onward, next_swap = steps[here + 4], steps[here + 5]
    next_branch[0] = steps[here + 6]
    loads = [
        pltpu.make_async_copy(src, peer.at[place], arrived.at[k])
        for k, (src, place) in enumerate(((ahead, swap), (behind, 1 - swap)))
    ]
    for load in loads:
        load.start()

    @pl.when(onward == 0)
    def _():
        lay_out(next_swap, cap, pic, next_ahead, next_behind, sent)

    for load in loads:
        load.wait()

    @pl.when(onward != 0)
    def _():
        lay_out(next_swap, peer.at[0], peer.at[1], next_ahead, next_behind, sent)

    @pl.when(partner < ROUNDS)
    def _():
        keeps = []
        for k, (left, out) in enumerate(((pic, pic_parts), (cap, cap_parts))):
            for first in range(0, left.shape[0], HALF):
                rows = slice(first, first + HALF)
                odds = jnp.exp(scores(left[rows, :], peer[k], sharp[0], shift[0]))
                coeff = (sharp[0] * odds_ratio(odds)).astype(jnp.bfloat16)
                if k == 0:
                    loss[rows, :] = folded(log_total(odds))
                part[k, rows, :] = product(coeff, peer[k]).astype(jnp.bfloat16)
                keeps.append(
                    pltpu.make_async_copy(part.at[k, rows], out.at[partner, rows], kept.at[len(keeps)])
                )
                keeps[-1].start()
        keeps.append(pltpu.make_async_copy(loss, losses.at[partner], kept.at[len(keeps)]))
        keeps[-1].start()
        for keep in keeps:
            keep.wait()

    wait_for_layout(cap, pic, next_ahead, next_behind, sent)


def last_kernel(
    mean_of, sharp, shift, pic, cap, pic_parts, cap_parts, losses, raw_pic, raw_cap, pic_factor, cap_factor,
    pic_grad, cap_grad, loss, raw, parts, lost, grads, arrived, sent,
):
    rows = pic.shape[0]
    loads = [
        pltpu.make_async_copy(src, out, arrived.at[k])
        for k, (src, out) in enumerate((
            (pic_parts, parts.at[0]), (raw_pic, raw.at[0]), (cap_parts, parts.at[1]), (raw_cap, raw.at[1]),
            (losses, lost),
        ))
    ]
    for load in loads:
        load.start()
    columns_at = lax.broadcasted_iota(jnp.int32, (HALF, rows), 1)
    rows_at = lax.broadcasted_iota(jnp.int32, (HALF, rows), 0)
    stores, own_loss = [], []
    for side, (left, right, factor, grad) in enumerate(
        ((pic, cap, pic_factor, pic_grad), (cap, pic, cap_factor, cap_grad))
    ):
        for first in range(0, rows, HALF):
            here = slice(first, first + HALF)
            logits = scores(left[here, :], right[...], sharp[0], shift[0])
            odds = jnp.exp(logits)
            label = jnp.where(rows_at + first == columns_at, 1.0, 0.0)
            if side == 0:
                own_loss.append(folded(log_total(odds) - label * logits))
            coeff = (sharp[0] * (odds_ratio(odds) - label)).astype(jnp.bfloat16)
            grads[side, here, :] = product(coeff, right[...])
            if first == 0:
                loads[2 * side].wait()
                loads[2 * side + 1].wait()
            wide = raw[side, here, :].astype(jnp.float32)
            scale = factor[here, :]
            total = grads[side, here, :] + sum(parts[side, r, here, :].astype(jnp.float32) for r in range(ROUNDS))
            inner = jnp.sum(wide * total, axis=-1, keepdims=True)
            grads[side, here, :] = scale * total - wide * (scale * scale * scale * inner)
            stores.append(pltpu.make_async_copy(grads.at[side, here], grad.at[here], sent.at[len(stores)]))
            stores[-1].start()
    loads[4].wait()
    ones = jnp.full((8, LANES), 1.0, jnp.float32)
    total = lax.dot_general(
        ones, jnp.concatenate(own_loss, axis=0) + sum(lost[r] for r in range(ROUNDS)), (((1,), (1,)), ((), ())),
        precision=lax.Precision.HIGHEST, preferred_element_type=jnp.float32,
    )
    loss[...] = total[0:1, :] * (1.0 / mean_of)
    for store in stores:
        store.wait()


def step_tile(step, steps, sharp, shift, pic, cap, ahead, behind, *parts):
    rows, width = pic.shape
    smem = pl.BlockSpec(memory_space=pltpu.SMEM)
    vmem = pl.BlockSpec(memory_space=pltpu.VMEM)
    somewhere = pl.BlockSpec(memory_space=pl.ANY)
    unit = jax.ShapeDtypeStruct((rows, width), jnp.bfloat16)
    return pl.pallas_call(
        step_kernel,
        out_shape=(
            *[jax.ShapeDtypeStruct(p.shape, p.dtype) for p in parts], unit, unit, jax.ShapeDtypeStruct((1,), jnp.int32)
        ),
        in_specs=[smem] * 4 + [vmem] * 2 + [somewhere] * 5,
        out_specs=(*[somewhere] * 3, vmem, vmem, smem),
        scratch_shapes=[
            pltpu.VMEM((2, rows, width), jnp.bfloat16),
            pltpu.VMEM((2, rows, width), jnp.bfloat16),
            pltpu.VMEM((rows, LANES), jnp.float32),
            pltpu.SemaphoreType.DMA((2,)),
            pltpu.SemaphoreType.DMA((2,)),
            pltpu.SemaphoreType.DMA((2 * rows // HALF + 1,)),
        ],
        input_output_aliases={8: 0, 9: 1, 10: 2},
        name="step_tile",
        compiler_params=pltpu.CompilerParams(vmem_limit_bytes=VMEM_LIMIT),
    )(step, steps, sharp, shift, pic, cap, ahead, behind, *parts)


def last_tile(mean_of, sharp, shift, pic, cap, parts, *rest):
    rows, width = pic.shape
    smem = pl.BlockSpec(memory_space=pltpu.SMEM)
    vmem = pl.BlockSpec(memory_space=pltpu.VMEM)
    somewhere = pl.BlockSpec(memory_space=pl.ANY)
    wide = jax.ShapeDtypeStruct((rows, width), jnp.float32)
    return pl.pallas_call(
        functools.partial(last_kernel, mean_of),
        out_shape=(wide, wide, jax.ShapeDtypeStruct((1, rows), jnp.float32)),
        in_specs=[smem, smem, vmem, vmem, *[somewhere] * 5, vmem, vmem],
        out_specs=(somewhere, somewhere, vmem),
        scratch_shapes=[
            pltpu.VMEM((2, rows, width), jnp.bfloat16),
            pltpu.VMEM((2, ROUNDS, rows, width), jnp.bfloat16),
            pltpu.VMEM((ROUNDS, rows, LANES), jnp.float32),
            pltpu.VMEM((2, rows, width), jnp.float32),
            pltpu.SemaphoreType.DMA((5,)),
            pltpu.SemaphoreType.DMA((2 * rows // HALF,)),
        ],
        compiler_params=pltpu.CompilerParams(vmem_limit_bytes=VMEM_LIMIT),
        name="last_tile",
    )(sharp, shift, pic, cap, *parts, *rest)


def shards(picture_raw_features, caption_raw_features, peer_assignment, sharpness_factor, offset_term):
    size = peer_assignment.shape[1]
    rows = picture_raw_features.shape[0]
    steps, branch, pic, cap, ahead, behind, pic_factor, cap_factor, *parts = start(
        peer_assignment, picture_raw_features, caption_raw_features
    )
    scalars = sharpness_factor, offset_term

    def one_step(step, carry):
        branch, ahead, behind, *parts = carry
        ahead, behind = move(branch[0], ahead, behind, size)
        *parts, ahead, behind, branch = step_tile(step.reshape(1), steps, *scalars, pic, cap, ahead, behind, *parts)
        return branch, ahead, behind, *parts

    _, _, _, *parts = lax.fori_loop(0, steps[FIELDS * ROWS_OF_PLAN], one_step, (branch, ahead, behind, *parts))
    image_embedding_gradient, grad_text, row_loss = last_tile(
        (ROUNDS + 1) * rows, *scalars, pic, cap, parts, picture_raw_features, caption_raw_features, pic_factor, cap_factor
    )
    return image_embedding_gradient, grad_text, row_loss.reshape(rows)


def solution(mesh):
    placed = (P(AXES, None), P(AXES, None), P(), P(), P())
    return jax.shard_map(
        shards,
        mesh=mesh,
        in_specs=placed,
        out_specs=(P(AXES, None), P(AXES, None), P(AXES)),
        check_vma=False,
    )
```

```python
import functools
import itertools

import jax
import jax.numpy as jnp
import numpy as np
from jax import lax
from jax.experimental import pallas as pl
from jax.experimental.pallas import tpu as pltpu
from jax.sharding import PartitionSpec as P

AXES = ("gx", "gy")
HALF = 256
LANES = 128
FIELDS = 4
ROWS_OF_PLAN = 8
ROUNDS = 3
VMEM_LIMIT = 40 * 2**20

DISTANCES = (
    1, 2, 3, 4, 5, 7, 8, 9, 10, 11, 12, 13, 14, 15, 16, 17, 18, 19, 20, 21, 22, 24, 25, 27, 28, 29, 31, 32, 33, 34,
    35, 36, 37, 39, 43, 44, 45, 47, 48, 53, 55, 56, 58, 59, 60, 61, 63, 64,
)
STEP_COST = (
    40, 58, 45, 42, 53, 63, 65, 54, 65, 57, 61, 50, 60, 42, 59, 45, 63, 46, 56, 53, 68, 64, 58, 54, 48, 47, 39, 41,
    44, 64, 52, 56, 67, 60, 65, 70, 65, 68, 70, 65, 58, 66, 71, 58, 65, 60, 61, 60,
)
STEP_OVERHEAD = 10


def route_tables(size):
    direct = np.full(size, 10**6)
    direct[0] = 0
    for distance, cost in zip(DISTANCES, STEP_COST):
        direct[distance] = direct[-distance % size] = cost + STEP_OVERHEAD
    cost, first = direct.copy(), np.arange(size)
    for step in range(1, size):
        by_two = direct[step] + np.roll(direct, step)
        first = np.where(by_two < cost, step, first)
        cost = np.minimum(cost, by_two)
    assert cost.max() < 10**6
    branch = np.zeros(size // 2 + 1, np.int32)
    branch[list(DISTANCES)] = np.arange(len(DISTANCES))
    table = np.zeros((3, size), np.int32)
    table[0], table[1], table[2, : branch.size] = cost, first, branch
    return table


def plan(peers, table, out):
    size = peers.shape[1]
    node = [peers[r, 0] for r in range(ROUNDS)]

    def wrapped(gap):
        return jnp.where(gap < 0, gap + size, gap)

    best = None
    for order in itertools.permutations(range(ROUNDS)):
        total, fields = None, []
        for place, r in enumerate(order):
            gap, onward = node[r], jnp.int32(0)
            if place:
                other = wrapped(node[r] - node[order[place - 1]])
                onward = jnp.where(table[0, other] < table[0, gap], 1, 0)
                gap = jnp.where(onward == 1, other, gap)
            total = table[0, gap] if total is None else total + table[0, gap]
            fields += [gap, onward]
        if best is None:
            best, kept = total, fields
        else:
            better = total < best
            best = jnp.where(better, total, best)
            kept = [jnp.where(better, n, o) for n, o in zip(fields, kept)]

    def emit(row, onward, gap, partner):
        out[FIELDS * row] = onward
        out[FIELDS * row + 1] = jnp.where(gap > size // 2, 1, 0)
        out[FIELDS * row + 2] = table[2, jnp.minimum(gap, size - gap)]
        out[FIELDS * row + 3] = partner

    row = jnp.int32(0)
    for r in range(ROUNDS):
        gap, onward = kept[2 * r], kept[2 * r + 1]
        step = table[1, gap]
        double = jnp.where(step == gap, 0, 1)
        emit(row, onward, step, jnp.where(double == 1, ROUNDS, r))
        emit(row + double, jnp.where(double == 1, 1, onward), wrapped(gap - step + step * (1 - double)), r)
        row = row + 1 + double
    emit(row, jnp.int32(0), jnp.int32(1), jnp.int32(ROUNDS))
    out[FIELDS * ROWS_OF_PLAN] = row


def start_kernel(
    peers, table, raw_pic, raw_cap,
    steps, first_branch, pic, cap, ahead, behind, pic_factor, cap_factor, pic_parts, cap_parts, losses,
    raw, unit, arrived, sent,
):
    loads = [pltpu.make_async_copy(src, raw.at[k], arrived.at[k]) for k, src in enumerate((raw_cap, raw_pic))]
    for load in loads:
        load.start()
    plan(peers, table, steps)
    first_branch[0] = steps[2]
    swap = steps[1]
    for k, factor in enumerate((cap_factor, pic_factor)):
        loads[k].wait()
        wide = raw[k].astype(jnp.float32)
        scale = lax.rsqrt(jnp.sum(wide * wide, axis=-1, keepdims=True) + 1e-06)
        unit[k] = (wide * scale).astype(jnp.bfloat16)
        factor[...] = scale
    stores = [
        pltpu.make_async_copy(unit.at[place], out, sent.at[k])
        for k, (place, out) in enumerate(((swap, ahead), (1 - swap, behind), (0, cap), (1, pic)))
    ]
    for store in stores:
        store.start()
    for store in stores:
        store.wait()


def start(peers, pic, cap):
    rows, width = pic.shape
    smem = pl.BlockSpec(memory_space=pltpu.SMEM)
    vmem = pl.BlockSpec(memory_space=pltpu.VMEM)
    somewhere = pl.BlockSpec(memory_space=pl.ANY)
    unit = jax.ShapeDtypeStruct((rows, width), jnp.bfloat16)
    factor = jax.ShapeDtypeStruct((rows, 1), jnp.float32)
    parts = jax.ShapeDtypeStruct((ROUNDS, rows, width), jnp.bfloat16)
    fields = jax.ShapeDtypeStruct((FIELDS * ROWS_OF_PLAN + 1,), jnp.int32)
    return pl.pallas_call(
        start_kernel,
        out_shape=(
            fields, jax.ShapeDtypeStruct((1,), jnp.int32), unit, unit, unit, unit, factor, factor, parts, parts,
            jax.ShapeDtypeStruct((ROUNDS, rows, LANES), jnp.float32),
        ),
        in_specs=[smem, smem, somewhere, somewhere],
        out_specs=(smem, smem, *[somewhere] * 4, vmem, vmem, *[somewhere] * 3),
        scratch_shapes=[
            pltpu.VMEM((2, rows, width), jnp.bfloat16),
            pltpu.VMEM((2, rows, width), jnp.bfloat16),
            pltpu.SemaphoreType.DMA((2,)),
            pltpu.SemaphoreType.DMA((4,)),
        ],
        compiler_params=pltpu.CompilerParams(vmem_limit_bytes=VMEM_LIMIT),
        name="start",
    )(peers, jnp.asarray(route_tables(peers.shape[1])), pic, cap)


def shifted(x, by, size):
    return lax.ppermute(x, AXES, [(i, (i + by) % size) for i in range(size)])


def move(branch, ahead, behind, size):
    def mover(by):
        return lambda a, b: (shifted(b, by, size), shifted(a, -by, size))

    behind, ahead = lax.switch(branch, [mover(by) for by in DISTANCES], ahead, behind)
    return ahead, behind


def scores(left, right, sharp, shift):
    dots = lax.dot_general(left, right, (((1,), (1,)), ((), ())), preferred_element_type=jnp.float32)
    return sharp * dots + shift


def odds_ratio(odds):
    total = 1.0 + odds
    guess = pl.reciprocal(total, approx=True)
    return odds * (guess * (2.0 - total * guess))


def log_total(odds):
    return jnp.where(odds < 1e-3, odds - 0.5 * odds * odds, jnp.log(1.0 + odds))


def folded(wide):
    return sum(wide[:, k : k + LANES] for k in range(0, wide.shape[1], LANES))


def product(coeff, entries):
    return lax.dot_general(coeff, entries, (((1,), (0,)), ((), ())), preferred_element_type=jnp.float32)


def step_kernel(
    step, steps, sharp, shift, pic, cap, ahead, behind, old_pic_parts, old_cap_parts, old_losses,
    pic_parts, cap_parts, losses, next_ahead, next_behind, next_branch,
    held, part, loss, arrived, sent, kept,
):
    here = FIELDS * step[0]
    swap, partner = steps[here + 1], steps[here + 3]
    onward, next_swap = steps[here + 4], steps[here + 5]
    next_branch[0] = steps[here + 6]
    loads = [
        pltpu.make_async_copy(src, held.at[place], arrived.at[k])
        for k, (src, place) in enumerate(((ahead, 2 + swap), (behind, 3 - swap), (pic, 1), (cap, 0)))
    ]
    for load in loads:
        load.start()
    for load in loads:
        load.wait()
    stores = [
        pltpu.make_async_copy(held.at[2 * onward + place], out, sent.at[k])
        for k, (out, place) in enumerate(((next_ahead, next_swap), (next_behind, 1 - next_swap)))
    ]
    for store in stores:
        store.start()

    @pl.when(partner < ROUNDS)
    def _():
        keeps = []
        for k, (left, right, out) in enumerate(((1, 2, pic_parts), (0, 3, cap_parts))):
            for first in range(0, held.shape[1], HALF):
                rows = slice(first, first + HALF)
                odds = jnp.exp(scores(held[left, rows, :], held[right], sharp[0], shift[0]))
                coeff = (sharp[0] * odds_ratio(odds)).astype(jnp.bfloat16)
                if k == 0:
                    loss[rows, :] = folded(log_total(odds))
                part[k, rows, :] = product(coeff, held[right]).astype(jnp.bfloat16)
                keeps.append(
                    pltpu.make_async_copy(part.at[k, rows], out.at[partner, rows], kept.at[len(keeps)])
                )
                keeps[-1].start()
        keeps.append(pltpu.make_async_copy(loss, losses.at[partner], kept.at[len(keeps)]))
        keeps[-1].start()
        for keep in keeps:
            keep.wait()

    for store in stores:
        store.wait()


def last_kernel(
    mean_of, sharp, shift, pic, cap, pic_parts, cap_parts, losses, raw_pic, raw_cap, pic_factor, cap_factor,
    pic_grad, cap_grad, loss, held, raw, parts, lost, grads, arrived, sent,
):
    rows = held.shape[1]
    loads = [
        pltpu.make_async_copy(src, out, arrived.at[k])
        for k, (src, out) in enumerate((
            (pic, held.at[1]), (cap, held.at[0]), (pic_parts, parts.at[0]), (raw_pic, raw.at[0]),
            (cap_parts, parts.at[1]), (raw_cap, raw.at[1]), (losses, lost),
        ))
    ]
    for load in loads:
        load.start()
    loads[0].wait()
    loads[1].wait()
    columns_at = lax.broadcasted_iota(jnp.int32, (HALF, rows), 1)
    rows_at = lax.broadcasted_iota(jnp.int32, (HALF, rows), 0)
    stores, own_loss = [], []
    for side, (factor, grad) in enumerate(((pic_factor, pic_grad), (cap_factor, cap_grad))):
        for first in range(0, rows, HALF):
            here = slice(first, first + HALF)
            logits = scores(held[1 - side, here, :], held[side], sharp[0], shift[0])
            odds = jnp.exp(logits)
            label = jnp.where(rows_at + first == columns_at, 1.0, 0.0)
            if side == 0:
                own_loss.append(folded(log_total(odds) - label * logits))
            coeff = (sharp[0] * (odds_ratio(odds) - label)).astype(jnp.bfloat16)
            grads[side, here, :] = product(coeff, held[side])
            if first == 0:
                loads[2 + 2 * side].wait()
                loads[3 + 2 * side].wait()
            wide = raw[side, here, :].astype(jnp.float32)
            scale = factor[here, :]
            total = grads[side, here, :] + sum(parts[side, r, here, :].astype(jnp.float32) for r in range(ROUNDS))
            inner = jnp.sum(wide * total, axis=-1, keepdims=True)
            grads[side, here, :] = scale * total - wide * (scale * scale * scale * inner)
            stores.append(pltpu.make_async_copy(grads.at[side, here], grad.at[here], sent.at[len(stores)]))
            stores[-1].start()
    loads[6].wait()
    ones = jnp.full((8, LANES), 1.0, jnp.float32)
    total = lax.dot_general(
        ones, jnp.concatenate(own_loss, axis=0) + sum(lost[r] for r in range(ROUNDS)), (((1,), (1,)), ((), ())),
        precision=lax.Precision.HIGHEST, preferred_element_type=jnp.float32,
    )
    loss[...] = total[0:1, :] * (1.0 / mean_of)
    for store in stores:
        store.wait()


def step_tile(step, steps, sharp, shift, pic, cap, ahead, behind, *parts):
    rows, width = pic.shape
    smem = pl.BlockSpec(memory_space=pltpu.SMEM)
    somewhere = pl.BlockSpec(memory_space=pl.ANY)
    unit = jax.ShapeDtypeStruct((rows, width), jnp.bfloat16)
    return pl.pallas_call(
        step_kernel,
        out_shape=(
            *[jax.ShapeDtypeStruct(p.shape, p.dtype) for p in parts], unit, unit, jax.ShapeDtypeStruct((1,), jnp.int32)
        ),
        in_specs=[smem] * 4 + [somewhere] * 7,
        out_specs=(*[somewhere] * 5, smem),
        scratch_shapes=[
            pltpu.VMEM((4, rows, width), jnp.bfloat16),
            pltpu.VMEM((2, rows, width), jnp.bfloat16),
            pltpu.VMEM((rows, LANES), jnp.float32),
            pltpu.SemaphoreType.DMA((4,)),
            pltpu.SemaphoreType.DMA((2,)),
            pltpu.SemaphoreType.DMA((2 * rows // HALF + 1,)),
        ],
        input_output_aliases={8: 0, 9: 1, 10: 2},
        name="step_tile",
        compiler_params=pltpu.CompilerParams(vmem_limit_bytes=VMEM_LIMIT),
    )(step, steps, sharp, shift, pic, cap, ahead, behind, *parts)


def last_tile(mean_of, sharp, shift, pic, cap, parts, *rest):
    rows, width = pic.shape
    smem = pl.BlockSpec(memory_space=pltpu.SMEM)
    vmem = pl.BlockSpec(memory_space=pltpu.VMEM)
    somewhere = pl.BlockSpec(memory_space=pl.ANY)
    wide = jax.ShapeDtypeStruct((rows, width), jnp.float32)
    return pl.pallas_call(
        functools.partial(last_kernel, mean_of),
        out_shape=(wide, wide, jax.ShapeDtypeStruct((1, rows), jnp.float32)),
        in_specs=[smem, smem, *[somewhere] * 7, vmem, vmem],
        out_specs=(somewhere, somewhere, vmem),
        scratch_shapes=[
            pltpu.VMEM((2, rows, width), jnp.bfloat16),
            pltpu.VMEM((2, rows, width), jnp.bfloat16),
            pltpu.VMEM((2, ROUNDS, rows, width), jnp.bfloat16),
            pltpu.VMEM((ROUNDS, rows, LANES), jnp.float32),
            pltpu.VMEM((2, rows, width), jnp.float32),
            pltpu.SemaphoreType.DMA((7,)),
            pltpu.SemaphoreType.DMA((2 * rows // HALF,)),
        ],
        compiler_params=pltpu.CompilerParams(vmem_limit_bytes=VMEM_LIMIT),
        name="last_tile",
    )(sharp, shift, pic, cap, *parts, *rest)


def shards(picture_raw_features, caption_raw_features, peer_assignment, sharpness_factor, offset_term):
    size = peer_assignment.shape[1]
    rows = picture_raw_features.shape[0]
    steps, branch, pic, cap, ahead, behind, pic_factor, cap_factor, *parts = start(
        peer_assignment, picture_raw_features, caption_raw_features
    )
    scalars = sharpness_factor, offset_term

    def one_step(step, carry):
        branch, ahead, behind, *parts = carry
        ahead, behind = move(branch[0], ahead, behind, size)
        *parts, ahead, behind, branch = step_tile(step.reshape(1), steps, *scalars, pic, cap, ahead, behind, *parts)
        return branch, ahead, behind, *parts

    _, _, _, *parts = lax.fori_loop(0, steps[FIELDS * ROWS_OF_PLAN], one_step, (branch, ahead, behind, *parts))
    image_embedding_gradient, grad_text, row_loss = last_tile(
        (ROUNDS + 1) * rows, *scalars, pic, cap, parts, picture_raw_features, caption_raw_features, pic_factor, cap_factor
    )
    return image_embedding_gradient, grad_text, row_loss.reshape(rows)


def solution(mesh):
    placed = (P(AXES, None), P(AXES, None), P(), P(), P())
    return jax.shard_map(
        shards,
        mesh=mesh,
        in_specs=placed,
        out_specs=(P(AXES, None), P(AXES, None), P(AXES)),
        check_vma=False,
    )
```

```python
import functools
import itertools

import jax
import jax.numpy as jnp
import numpy as np
from jax import lax
from jax.experimental import pallas as pl
from jax.experimental.pallas import tpu as pltpu
from jax.sharding import PartitionSpec as P

AXES = ("gx", "gy")
HALF = 256
LANES = 128
FIELDS = 4
ROWS_OF_PLAN = 8
ROUNDS = 3
VMEM_LIMIT = 40 * 2**20

DISTANCES = (
    1, 2, 3, 4, 5, 7, 9, 10, 11, 12, 13, 14, 15, 16, 17, 18, 19, 20, 21, 24, 25, 27, 28, 29, 31, 32, 33, 34, 35, 36,
    37, 39, 43, 44, 45, 53, 55, 56, 60, 61,
)
STEP_COST = (
    40, 58, 45, 42, 53, 63, 54, 65, 57, 61, 50, 60, 42, 59, 45, 63, 46, 56, 53, 64, 58, 54, 48, 47, 39, 41, 44, 64,
    52, 56, 67, 60, 65, 70, 65, 65, 58, 66, 65, 60,
)
STEP_OVERHEAD = 10


def route_tables(size):
    direct = np.full(size, 10**6)
    direct[0] = 0
    for distance, cost in zip(DISTANCES, STEP_COST):
        direct[distance] = direct[-distance % size] = cost + STEP_OVERHEAD
    cost, first = direct.copy(), np.arange(size)
    for step in range(1, size):
        by_two = direct[step] + np.roll(direct, step)
        first = np.where(by_two < cost, step, first)
        cost = np.minimum(cost, by_two)
    assert cost.max() < 10**6
    branch = np.zeros(size // 2 + 1, np.int32)
    branch[list(DISTANCES)] = np.arange(len(DISTANCES))
    table = np.zeros((3, size), np.int32)
    table[0], table[1], table[2, : branch.size] = cost, first, branch
    return table


def plan(peers, table, out):
    size = peers.shape[1]
    node = [peers[r, 0] for r in range(ROUNDS)]

    def wrapped(gap):
        return jnp.where(gap < 0, gap + size, gap)

    best = None
    for order in itertools.permutations(range(ROUNDS)):
        total, fields = None, []
        for place, r in enumerate(order):
            gap, onward = node[r], jnp.int32(0)
            if place:
                other = wrapped(node[r] - node[order[place - 1]])
                onward = jnp.where(table[0, other] < table[0, gap], 1, 0)
                gap = jnp.where(onward == 1, other, gap)
            total = table[0, gap] if total is None else total + table[0, gap]
            fields += [gap, onward]
        if best is None:
            best, kept = total, fields
        else:
            better = total < best
            best = jnp.where(better, total, best)
            kept = [jnp.where(better, n, o) for n, o in zip(fields, kept)]

    def emit(row, onward, gap, partner):
        out[FIELDS * row] = onward
        out[FIELDS * row + 1] = jnp.where(gap > size // 2, 1, 0)
        out[FIELDS * row + 2] = table[2, jnp.minimum(gap, size - gap)]
        out[FIELDS * row + 3] = partner

    row = jnp.int32(0)
    for r in range(ROUNDS):
        gap, onward = kept[2 * r], kept[2 * r + 1]
        step = table[1, gap]
        double = jnp.where(step == gap, 0, 1)
        emit(row, onward, step, jnp.where(double == 1, ROUNDS, r))
        emit(row + double, jnp.where(double == 1, 1, onward), wrapped(gap - step + step * (1 - double)), r)
        row = row + 1 + double
    emit(row, jnp.int32(0), jnp.int32(1), jnp.int32(ROUNDS))
    out[FIELDS * ROWS_OF_PLAN] = row


def start_kernel(
    peers, table, raw_pic, raw_cap,
    steps, first_branch, pic, cap, ahead, behind, pic_factor, cap_factor, pic_parts, cap_parts, losses,
    raw, unit, arrived, sent,
):
    loads = [pltpu.make_async_copy(src, raw.at[k], arrived.at[k]) for k, src in enumerate((raw_cap, raw_pic))]
    for load in loads:
        load.start()
    plan(peers, table, steps)
    first_branch[0] = steps[2]
    swap = steps[1]
    for k, factor in enumerate((cap_factor, pic_factor)):
        loads[k].wait()
        wide = raw[k].astype(jnp.float32)
        scale = lax.rsqrt(jnp.sum(wide * wide, axis=-1, keepdims=True) + 1e-06)
        unit[k] = (wide * scale).astype(jnp.bfloat16)
        factor[...] = scale
    stores = [
        pltpu.make_async_copy(unit.at[place], out, sent.at[k])
        for k, (place, out) in enumerate(((swap, ahead), (1 - swap, behind), (0, cap), (1, pic)))
    ]
    for store in stores:
        store.start()
    for store in stores:
        store.wait()


def start(peers, pic, cap):
    rows, width = pic.shape
    smem = pl.BlockSpec(memory_space=pltpu.SMEM)
    vmem = pl.BlockSpec(memory_space=pltpu.VMEM)
    somewhere = pl.BlockSpec(memory_space=pl.ANY)
    unit = jax.ShapeDtypeStruct((rows, width), jnp.bfloat16)
    factor = jax.ShapeDtypeStruct((rows, 1), jnp.float32)
    parts = jax.ShapeDtypeStruct((ROUNDS, rows, width), jnp.bfloat16)
    fields = jax.ShapeDtypeStruct((FIELDS * ROWS_OF_PLAN + 1,), jnp.int32)
    return pl.pallas_call(
        start_kernel,
        out_shape=(
            fields, jax.ShapeDtypeStruct((1,), jnp.int32), unit, unit, unit, unit, factor, factor, parts, parts,
            jax.ShapeDtypeStruct((ROUNDS, rows, LANES), jnp.float32),
        ),
        in_specs=[smem, smem, somewhere, somewhere],
        out_specs=(smem, smem, *[somewhere] * 4, vmem, vmem, *[somewhere] * 3),
        scratch_shapes=[
            pltpu.VMEM((2, rows, width), jnp.bfloat16),
            pltpu.VMEM((2, rows, width), jnp.bfloat16),
            pltpu.SemaphoreType.DMA((2,)),
            pltpu.SemaphoreType.DMA((4,)),
        ],
        compiler_params=pltpu.CompilerParams(vmem_limit_bytes=VMEM_LIMIT),
        name="start",
    )(peers, jnp.asarray(route_tables(peers.shape[1])), pic, cap)


def shifted(x, by, size):
    return lax.ppermute(x, AXES, [(i, (i + by) % size) for i in range(size)])


def move(branch, ahead, behind, size):
    def mover(by):
        return lambda a, b: (shifted(b, by, size), shifted(a, -by, size))

    behind, ahead = lax.switch(branch, [mover(by) for by in DISTANCES], ahead, behind)
    return ahead, behind


def scores(left, right, sharp, shift):
    dots = lax.dot_general(left, right, (((1,), (1,)), ((), ())), preferred_element_type=jnp.float32)
    return sharp * dots + shift


def odds_ratio(odds):
    total = 1.0 + odds
    guess = pl.reciprocal(total, approx=True)
    return odds * (guess * (2.0 - total * guess))


def log_total(odds):
    return jnp.where(odds < 1e-3, odds - 0.5 * odds * odds, jnp.log(1.0 + odds))


def folded(wide):
    return sum(wide[:, k : k + LANES] for k in range(0, wide.shape[1], LANES))


def product(coeff, entries):
    return lax.dot_general(coeff, entries, (((1,), (0,)), ((), ())), preferred_element_type=jnp.float32)


def step_kernel(
    step, steps, sharp, shift, pic, cap, ahead, behind, old_pic_parts, old_cap_parts, old_losses,
    pic_parts, cap_parts, losses, next_ahead, next_behind, next_branch,
    held, part, loss, arrived, sent, kept,
):
    here = FIELDS * step[0]
    swap, partner = steps[here + 1], steps[here + 3]
    onward, next_swap = steps[here + 4], steps[here + 5]
    next_branch[0] = steps[here + 6]
    loads = [
        pltpu.make_async_copy(src, held.at[place], arrived.at[k])
        for k, (src, place) in enumerate(((ahead, 2 + swap), (behind, 3 - swap), (pic, 1), (cap, 0)))
    ]
    for load in loads:
        load.start()
    for load in loads:
        load.wait()
    stores = [
        pltpu.make_async_copy(held.at[2 * onward + place], out, sent.at[k])
        for k, (out, place) in enumerate(((next_ahead, next_swap), (next_behind, 1 - next_swap)))
    ]
    for store in stores:
        store.start()

    @pl.when(partner < ROUNDS)
    def _():
        keeps = []
        for k, (left, right, out) in enumerate(((1, 2, pic_parts), (0, 3, cap_parts))):
            for first in range(0, held.shape[1], HALF):
                rows = slice(first, first + HALF)
                odds = jnp.exp(scores(held[left, rows, :], held[right], sharp[0], shift[0]))
                coeff = (sharp[0] * odds_ratio(odds)).astype(jnp.bfloat16)
                if k == 0:
                    loss[rows, :] = folded(log_total(odds))
                part[k, rows, :] = product(coeff, held[right]).astype(jnp.bfloat16)
                keeps.append(
                    pltpu.make_async_copy(part.at[k, rows], out.at[partner, rows], kept.at[len(keeps)])
                )
                keeps[-1].start()
        keeps.append(pltpu.make_async_copy(loss, losses.at[partner], kept.at[len(keeps)]))
        keeps[-1].start()
        for keep in keeps:
            keep.wait()

    for store in stores:
        store.wait()


def last_kernel(
    mean_of, sharp, shift, pic, cap, pic_parts, cap_parts, losses, raw_pic, raw_cap, pic_factor, cap_factor,
    pic_grad, cap_grad, loss, held, raw, parts, lost, grads, arrived, sent,
):
    rows = held.shape[1]
    loads = [
        pltpu.make_async_copy(src, out, arrived.at[k])
        for k, (src, out) in enumerate((
            (pic, held.at[1]), (cap, held.at[0]), (pic_parts, parts.at[0]), (raw_pic, raw.at[0]),
            (cap_parts, parts.at[1]), (raw_cap, raw.at[1]), (losses, lost),
        ))
    ]
    for load in loads:
        load.start()
    loads[0].wait()
    loads[1].wait()
    columns_at = lax.broadcasted_iota(jnp.int32, (HALF, rows), 1)
    rows_at = lax.broadcasted_iota(jnp.int32, (HALF, rows), 0)
    stores, own_loss = [], []
    for side, (factor, grad) in enumerate(((pic_factor, pic_grad), (cap_factor, cap_grad))):
        for first in range(0, rows, HALF):
            here = slice(first, first + HALF)
            logits = scores(held[1 - side, here, :], held[side], sharp[0], shift[0])
            odds = jnp.exp(logits)
            label = jnp.where(rows_at + first == columns_at, 1.0, 0.0)
            if side == 0:
                own_loss.append(folded(log_total(odds) - label * logits))
            coeff = (sharp[0] * (odds_ratio(odds) - label)).astype(jnp.bfloat16)
            grads[side, here, :] = product(coeff, held[side])
            if first == 0:
                loads[2 + 2 * side].wait()
                loads[3 + 2 * side].wait()
            wide = raw[side, here, :].astype(jnp.float32)
            scale = factor[here, :]
            total = grads[side, here, :] + sum(parts[side, r, here, :].astype(jnp.float32) for r in range(ROUNDS))
            inner = jnp.sum(wide * total, axis=-1, keepdims=True)
            grads[side, here, :] = scale * total - wide * (scale * scale * scale * inner)
            stores.append(pltpu.make_async_copy(grads.at[side, here], grad.at[here], sent.at[len(stores)]))
            stores[-1].start()
    loads[6].wait()
    ones = jnp.full((8, LANES), 1.0, jnp.float32)
    total = lax.dot_general(
        ones, jnp.concatenate(own_loss, axis=0) + sum(lost[r] for r in range(ROUNDS)), (((1,), (1,)), ((), ())),
        precision=lax.Precision.HIGHEST, preferred_element_type=jnp.float32,
    )
    loss[...] = total[0:1, :] * (1.0 / mean_of)
    for store in stores:
        store.wait()


def step_tile(step, steps, sharp, shift, pic, cap, ahead, behind, *parts):
    rows, width = pic.shape
    smem = pl.BlockSpec(memory_space=pltpu.SMEM)
    somewhere = pl.BlockSpec(memory_space=pl.ANY)
    unit = jax.ShapeDtypeStruct((rows, width), jnp.bfloat16)
    return pl.pallas_call(
        step_kernel,
        out_shape=(
            *[jax.ShapeDtypeStruct(p.shape, p.dtype) for p in parts], unit, unit, jax.ShapeDtypeStruct((1,), jnp.int32)
        ),
        in_specs=[smem] * 4 + [somewhere] * 7,
        out_specs=(*[somewhere] * 5, smem),
        scratch_shapes=[
            pltpu.VMEM((4, rows, width), jnp.bfloat16),
            pltpu.VMEM((2, rows, width), jnp.bfloat16),
            pltpu.VMEM((rows, LANES), jnp.float32),
            pltpu.SemaphoreType.DMA((4,)),
            pltpu.SemaphoreType.DMA((2,)),
            pltpu.SemaphoreType.DMA((2 * rows // HALF + 1,)),
        ],
        input_output_aliases={8: 0, 9: 1, 10: 2},
        name="step_tile",
        compiler_params=pltpu.CompilerParams(vmem_limit_bytes=VMEM_LIMIT),
    )(step, steps, sharp, shift, pic, cap, ahead, behind, *parts)


def last_tile(mean_of, sharp, shift, pic, cap, parts, *rest):
    rows, width = pic.shape
    smem = pl.BlockSpec(memory_space=pltpu.SMEM)
    vmem = pl.BlockSpec(memory_space=pltpu.VMEM)
    somewhere = pl.BlockSpec(memory_space=pl.ANY)
    wide = jax.ShapeDtypeStruct((rows, width), jnp.float32)
    return pl.pallas_call(
        functools.partial(last_kernel, mean_of),
        out_shape=(wide, wide, jax.ShapeDtypeStruct((1, rows), jnp.float32)),
        in_specs=[smem, smem, *[somewhere] * 7, vmem, vmem],
        out_specs=(somewhere, somewhere, vmem),
        scratch_shapes=[
            pltpu.VMEM((2, rows, width), jnp.bfloat16),
            pltpu.VMEM((2, rows, width), jnp.bfloat16),
            pltpu.VMEM((2, ROUNDS, rows, width), jnp.bfloat16),
            pltpu.VMEM((ROUNDS, rows, LANES), jnp.float32),
            pltpu.VMEM((2, rows, width), jnp.float32),
            pltpu.SemaphoreType.DMA((7,)),
            pltpu.SemaphoreType.DMA((2 * rows // HALF,)),
        ],
        compiler_params=pltpu.CompilerParams(vmem_limit_bytes=VMEM_LIMIT),
        name="last_tile",
    )(sharp, shift, pic, cap, *parts, *rest)


def shards(picture_raw_features, caption_raw_features, peer_assignment, sharpness_factor, offset_term):
    size = peer_assignment.shape[1]
    rows = picture_raw_features.shape[0]
    steps, branch, pic, cap, ahead, behind, pic_factor, cap_factor, *parts = start(
        peer_assignment, picture_raw_features, caption_raw_features
    )
    scalars = sharpness_factor, offset_term

    def one_step(step, carry):
        branch, ahead, behind, *parts = carry
        ahead, behind = move(branch[0], ahead, behind, size)
        *parts, ahead, behind, branch = step_tile(step.reshape(1), steps, *scalars, pic, cap, ahead, behind, *parts)
        return branch, ahead, behind, *parts

    _, _, _, *parts = lax.fori_loop(0, steps[FIELDS * ROWS_OF_PLAN], one_step, (branch, ahead, behind, *parts))
    image_embedding_gradient, grad_text, row_loss = last_tile(
        (ROUNDS + 1) * rows, *scalars, pic, cap, parts, picture_raw_features, caption_raw_features, pic_factor, cap_factor
    )
    return image_embedding_gradient, grad_text, row_loss.reshape(rows)


def solution(mesh):
    placed = (P(AXES, None), P(AXES, None), P(), P(), P())
    return jax.shard_map(
        shards,
        mesh=mesh,
        in_specs=placed,
        out_specs=(P(AXES, None), P(AXES, None), P(AXES)),
        check_vma=False,
    )
```

```python
import functools
import itertools

import jax
import jax.numpy as jnp
import numpy as np
from jax import lax
from jax.experimental import pallas as pl
from jax.experimental.pallas import tpu as pltpu
from jax.sharding import PartitionSpec as P

AXES = ("gx", "gy")
HALF = 256
LANES = 128
FIELDS = 4
ROWS_OF_PLAN = 8
ROUNDS = 3
VMEM_LIMIT = 40 * 2**20

DISTANCES = (
    1, 3, 4, 5, 7, 9, 10, 11, 12, 13, 14, 15, 16, 17, 18, 19, 20, 21, 25, 27, 28, 29, 31, 32, 33, 34, 35, 36, 37,
    39, 43, 44, 55, 56, 60, 61,
)
STEP_COST = (
    40, 45, 42, 53, 63, 54, 65, 57, 61, 50, 60, 42, 59, 45, 63, 46, 56, 53, 58, 54, 48, 47, 39, 41, 44, 64, 52, 56,
    67, 60, 65, 70, 58, 66, 65, 60,
)
STEP_OVERHEAD = 10


def route_tables(size):
    direct = np.full(size, 10**6)
    direct[0] = 0
    for distance, cost in zip(DISTANCES, STEP_COST):
        direct[distance] = direct[-distance % size] = cost + STEP_OVERHEAD
    cost, first = direct.copy(), np.arange(size)
    for step in range(1, size):
        by_two = direct[step] + np.roll(direct, step)
        first = np.where(by_two < cost, step, first)
        cost = np.minimum(cost, by_two)
    assert cost.max() < 10**6
    branch = np.zeros(size // 2 + 1, np.int32)
    branch[list(DISTANCES)] = np.arange(len(DISTANCES))
    table = np.zeros((3, size), np.int32)
    table[0], table[1], table[2, : branch.size] = cost, first, branch
    return table


def plan(peers, table, out):
    size = peers.shape[1]
    node = [peers[r, 0] for r in range(ROUNDS)]

    def wrapped(gap):
        return jnp.where(gap < 0, gap + size, gap)

    best = None
    for order in itertools.permutations(range(ROUNDS)):
        total, fields = None, []
        for place, r in enumerate(order):
            gap, onward = node[r], jnp.int32(0)
            if place:
                other = wrapped(node[r] - node[order[place - 1]])
                onward = jnp.where(table[0, other] < table[0, gap], 1, 0)
                gap = jnp.where(onward == 1, other, gap)
            total = table[0, gap] if total is None else total + table[0, gap]
            fields += [gap, onward]
        if best is None:
            best, kept = total, fields
        else:
            better = total < best
            best = jnp.where(better, total, best)
            kept = [jnp.where(better, n, o) for n, o in zip(fields, kept)]

    def emit(row, onward, gap, partner):
        out[FIELDS * row] = onward
        out[FIELDS * row + 1] = jnp.where(gap > size // 2, 1, 0)
        out[FIELDS * row + 2] = table[2, jnp.minimum(gap, size - gap)]
        out[FIELDS * row + 3] = partner

    row = jnp.int32(0)
    for r in range(ROUNDS):
        gap, onward = kept[2 * r], kept[2 * r + 1]
        step = table[1, gap]
        double = jnp.where(step == gap, 0, 1)
        emit(row, onward, step, jnp.where(double == 1, ROUNDS, r))
        emit(row + double, jnp.where(double == 1, 1, onward), wrapped(gap - step + step * (1 - double)), r)
        row = row + 1 + double
    emit(row, jnp.int32(0), jnp.int32(1), jnp.int32(ROUNDS))
    out[FIELDS * ROWS_OF_PLAN] = row


def start_kernel(
    peers, table, raw_pic, raw_cap,
    steps, first_branch, pic, cap, ahead, behind, pic_factor, cap_factor, pic_parts, cap_parts, losses,
    raw, unit, arrived, sent,
):
    loads = [pltpu.make_async_copy(src, raw.at[k], arrived.at[k]) for k, src in enumerate((raw_cap, raw_pic))]
    for load in loads:
        load.start()
    plan(peers, table, steps)
    first_branch[0] = steps[2]
    swap = steps[1]
    for k, factor in enumerate((cap_factor, pic_factor)):
        loads[k].wait()
        wide = raw[k].astype(jnp.float32)
        scale = lax.rsqrt(jnp.sum(wide * wide, axis=-1, keepdims=True) + 1e-06)
        unit[k] = (wide * scale).astype(jnp.bfloat16)
        factor[...] = scale
    stores = [
        pltpu.make_async_copy(unit.at[place], out, sent.at[k])
        for k, (place, out) in enumerate(((swap, ahead), (1 - swap, behind), (0, cap), (1, pic)))
    ]
    for store in stores:
        store.start()
    for store in stores:
        store.wait()


def start(peers, pic, cap):
    rows, width = pic.shape
    smem = pl.BlockSpec(memory_space=pltpu.SMEM)
    vmem = pl.BlockSpec(memory_space=pltpu.VMEM)
    somewhere = pl.BlockSpec(memory_space=pl.ANY)
    unit = jax.ShapeDtypeStruct((rows, width), jnp.bfloat16)
    factor = jax.ShapeDtypeStruct((rows, 1), jnp.float32)
    parts = jax.ShapeDtypeStruct((ROUNDS, rows, width), jnp.bfloat16)
    fields = jax.ShapeDtypeStruct((FIELDS * ROWS_OF_PLAN + 1,), jnp.int32)
    return pl.pallas_call(
        start_kernel,
        out_shape=(
            fields, jax.ShapeDtypeStruct((1,), jnp.int32), unit, unit, unit, unit, factor, factor, parts, parts,
            jax.ShapeDtypeStruct((ROUNDS, rows, LANES), jnp.float32),
        ),
        in_specs=[smem, smem, somewhere, somewhere],
        out_specs=(smem, smem, *[somewhere] * 4, vmem, vmem, *[somewhere] * 3),
        scratch_shapes=[
            pltpu.VMEM((2, rows, width), jnp.bfloat16),
            pltpu.VMEM((2, rows, width), jnp.bfloat16),
            pltpu.SemaphoreType.DMA((2,)),
            pltpu.SemaphoreType.DMA((4,)),
        ],
        compiler_params=pltpu.CompilerParams(vmem_limit_bytes=VMEM_LIMIT),
        name="start",
    )(peers, jnp.asarray(route_tables(peers.shape[1])), pic, cap)


def shifted(x, by, size):
    return lax.ppermute(x, AXES, [(i, (i + by) % size) for i in range(size)])


def move(branch, ahead, behind, size):
    def mover(by):
        return lambda a, b: (shifted(b, by, size), shifted(a, -by, size))

    behind, ahead = lax.switch(branch, [mover(by) for by in DISTANCES], ahead, behind)
    return ahead, behind


def scores(left, right, sharp, shift):
    dots = lax.dot_general(left, right, (((1,), (1,)), ((), ())), preferred_element_type=jnp.float32)
    return sharp * dots + shift


def odds_ratio(odds):
    total = 1.0 + odds
    guess = pl.reciprocal(total, approx=True)
    return odds * (guess * (2.0 - total * guess))


def log_total(odds):
    return jnp.where(odds < 1e-3, odds - 0.5 * odds * odds, jnp.log(1.0 + odds))


def folded(wide):
    return sum(wide[:, k : k + LANES] for k in range(0, wide.shape[1], LANES))


def product(coeff, entries):
    return lax.dot_general(coeff, entries, (((1,), (0,)), ((), ())), preferred_element_type=jnp.float32)


def step_kernel(
    step, steps, sharp, shift, pic, cap, ahead, behind, old_pic_parts, old_cap_parts, old_losses,
    pic_parts, cap_parts, losses, next_ahead, next_behind, next_branch,
    held, part, loss, arrived, sent, kept,
):
    here = FIELDS * step[0]
    swap, partner = steps[here + 1], steps[here + 3]
    onward, next_swap = steps[here + 4], steps[here + 5]
    next_branch[0] = steps[here + 6]
    loads = [
        pltpu.make_async_copy(src, held.at[place], arrived.at[k])
        for k, (src, place) in enumerate(((ahead, 2 + swap), (behind, 3 - swap), (pic, 1), (cap, 0)))
    ]
    for load in loads:
        load.start()
    for load in loads:
        load.wait()
    stores = [
        pltpu.make_async_copy(held.at[2 * onward + place], out, sent.at[k])
        for k, (out, place) in enumerate(((next_ahead, next_swap), (next_behind, 1 - next_swap)))
    ]
    for store in stores:
        store.start()

    @pl.when(partner < ROUNDS)
    def _():
        keeps = []
        for k, (left, right, out) in enumerate(((1, 2, pic_parts), (0, 3, cap_parts))):
            for first in range(0, held.shape[1], HALF):
                rows = slice(first, first + HALF)
                odds = jnp.exp(scores(held[left, rows, :], held[right], sharp[0], shift[0]))
                coeff = (sharp[0] * odds_ratio(odds)).astype(jnp.bfloat16)
                if k == 0:
                    loss[rows, :] = folded(log_total(odds))
                part[k, rows, :] = product(coeff, held[right]).astype(jnp.bfloat16)
                keeps.append(
                    pltpu.make_async_copy(part.at[k, rows], out.at[partner, rows], kept.at[len(keeps)])
                )
                keeps[-1].start()
        keeps.append(pltpu.make_async_copy(loss, losses.at[partner], kept.at[len(keeps)]))
        keeps[-1].start()
        for keep in keeps:
            keep.wait()

    for store in stores:
        store.wait()


def last_kernel(
    mean_of, sharp, shift, pic, cap, pic_parts, cap_parts, losses, raw_pic, raw_cap, pic_factor, cap_factor,
    pic_grad, cap_grad, loss, held, raw, parts, lost, grads, arrived, sent,
):
    rows = held.shape[1]
    loads = [
        pltpu.make_async_copy(src, out, arrived.at[k])
        for k, (src, out) in enumerate((
            (pic, held.at[1]), (cap, held.at[0]), (pic_parts, parts.at[0]), (raw_pic, raw.at[0]),
            (cap_parts, parts.at[1]), (raw_cap, raw.at[1]), (losses, lost),
        ))
    ]
    for load in loads:
        load.start()
    loads[0].wait()
    loads[1].wait()
    columns_at = lax.broadcasted_iota(jnp.int32, (HALF, rows), 1)
    rows_at = lax.broadcasted_iota(jnp.int32, (HALF, rows), 0)
    stores, own_loss = [], []
    for side, (factor, grad) in enumerate(((pic_factor, pic_grad), (cap_factor, cap_grad))):
        for first in range(0, rows, HALF):
            here = slice(first, first + HALF)
            logits = scores(held[1 - side, here, :], held[side], sharp[0], shift[0])
            odds = jnp.exp(logits)
            label = jnp.where(rows_at + first == columns_at, 1.0, 0.0)
            if side == 0:
                own_loss.append(folded(log_total(odds) - label * logits))
            coeff = (sharp[0] * (odds_ratio(odds) - label)).astype(jnp.bfloat16)
            grads[side, here, :] = product(coeff, held[side])
            if first == 0:
                loads[2 + 2 * side].wait()
                loads[3 + 2 * side].wait()
            wide = raw[side, here, :].astype(jnp.float32)
            scale = factor[here, :]
            total = grads[side, here, :] + sum(parts[side, r, here, :].astype(jnp.float32) for r in range(ROUNDS))
            inner = jnp.sum(wide * total, axis=-1, keepdims=True)
            grads[side, here, :] = scale * total - wide * (scale * scale * scale * inner)
            stores.append(pltpu.make_async_copy(grads.at[side, here], grad.at[here], sent.at[len(stores)]))
            stores[-1].start()
    loads[6].wait()
    ones = jnp.full((8, LANES), 1.0, jnp.float32)
    total = lax.dot_general(
        ones, jnp.concatenate(own_loss, axis=0) + sum(lost[r] for r in range(ROUNDS)), (((1,), (1,)), ((), ())),
        precision=lax.Precision.HIGHEST, preferred_element_type=jnp.float32,
    )
    loss[...] = total[0:1, :] * (1.0 / mean_of)
    for store in stores:
        store.wait()


def step_tile(step, steps, sharp, shift, pic, cap, ahead, behind, *parts):
    rows, width = pic.shape
    smem = pl.BlockSpec(memory_space=pltpu.SMEM)
    somewhere = pl.BlockSpec(memory_space=pl.ANY)
    unit = jax.ShapeDtypeStruct((rows, width), jnp.bfloat16)
    return pl.pallas_call(
        step_kernel,
        out_shape=(
            *[jax.ShapeDtypeStruct(p.shape, p.dtype) for p in parts], unit, unit, jax.ShapeDtypeStruct((1,), jnp.int32)
        ),
        in_specs=[smem] * 4 + [somewhere] * 7,
        out_specs=(*[somewhere] * 5, smem),
        scratch_shapes=[
            pltpu.VMEM((4, rows, width), jnp.bfloat16),
            pltpu.VMEM((2, rows, width), jnp.bfloat16),
            pltpu.VMEM((rows, LANES), jnp.float32),
            pltpu.SemaphoreType.DMA((4,)),
            pltpu.SemaphoreType.DMA((2,)),
            pltpu.SemaphoreType.DMA((2 * rows // HALF + 1,)),
        ],
        input_output_aliases={8: 0, 9: 1, 10: 2},
        name="step_tile",
        compiler_params=pltpu.CompilerParams(vmem_limit_bytes=VMEM_LIMIT),
    )(step, steps, sharp, shift, pic, cap, ahead, behind, *parts)


def last_tile(mean_of, sharp, shift, pic, cap, parts, *rest):
    rows, width = pic.shape
    smem = pl.BlockSpec(memory_space=pltpu.SMEM)
    vmem = pl.BlockSpec(memory_space=pltpu.VMEM)
    somewhere = pl.BlockSpec(memory_space=pl.ANY)
    wide = jax.ShapeDtypeStruct((rows, width), jnp.float32)
    return pl.pallas_call(
        functools.partial(last_kernel, mean_of),
        out_shape=(wide, wide, jax.ShapeDtypeStruct((1, rows), jnp.float32)),
        in_specs=[smem, smem, *[somewhere] * 7, vmem, vmem],
        out_specs=(somewhere, somewhere, vmem),
        scratch_shapes=[
            pltpu.VMEM((2, rows, width), jnp.bfloat16),
            pltpu.VMEM((2, rows, width), jnp.bfloat16),
            pltpu.VMEM((2, ROUNDS, rows, width), jnp.bfloat16),
            pltpu.VMEM((ROUNDS, rows, LANES), jnp.float32),
            pltpu.VMEM((2, rows, width), jnp.float32),
            pltpu.SemaphoreType.DMA((7,)),
            pltpu.SemaphoreType.DMA((2 * rows // HALF,)),
        ],
        compiler_params=pltpu.CompilerParams(vmem_limit_bytes=VMEM_LIMIT),
        name="last_tile",
    )(sharp, shift, pic, cap, *parts, *rest)


def shards(picture_raw_features, caption_raw_features, peer_assignment, sharpness_factor, offset_term):
    size = peer_assignment.shape[1]
    rows = picture_raw_features.shape[0]
    steps, branch, pic, cap, ahead, behind, pic_factor, cap_factor, *parts = start(
        peer_assignment, picture_raw_features, caption_raw_features
    )
    scalars = sharpness_factor, offset_term

    def one_step(step, carry):
        branch, ahead, behind, *parts = carry
        ahead, behind = move(branch[0], ahead, behind, size)
        *parts, ahead, behind, branch = step_tile(step.reshape(1), steps, *scalars, pic, cap, ahead, behind, *parts)
        return branch, ahead, behind, *parts

    _, _, _, *parts = lax.fori_loop(0, steps[FIELDS * ROWS_OF_PLAN], one_step, (branch, ahead, behind, *parts))
    image_embedding_gradient, grad_text, row_loss = last_tile(
        (ROUNDS + 1) * rows, *scalars, pic, cap, parts, picture_raw_features, caption_raw_features, pic_factor, cap_factor
    )
    return image_embedding_gradient, grad_text, row_loss.reshape(rows)


def solution(mesh):
    placed = (P(AXES, None), P(AXES, None), P(), P(), P())
    return jax.shard_map(
        shards,
        mesh=mesh,
        in_specs=placed,
        out_specs=(P(AXES, None), P(AXES, None), P(AXES)),
        check_vma=False,
    )
```

```python
import functools
import itertools

import jax
import jax.numpy as jnp
import numpy as np
from jax import lax
from jax.experimental import pallas as pl
from jax.experimental.pallas import tpu as pltpu
from jax.sharding import PartitionSpec as P

AXES = ("gx", "gy")
HALF = 256
LANES = 128
FIELDS = 4
ROWS_OF_PLAN = 8
ROUNDS = 3
VMEM_LIMIT = 40 * 2**20
START_VMEM_LIMIT = 60 * 2**20

DISTANCES = (
    1, 3, 4, 5, 7, 8, 9, 10, 11, 13, 14, 15, 16, 17, 18, 19, 20, 21, 24, 25, 27, 28, 29, 30, 31, 32, 33, 36, 40, 42,
    43, 45, 53, 55, 56, 57, 59, 60, 61,
)
STEP_COST = (
    35, 39, 40, 49, 58, 58, 50, 61, 50, 43, 56, 38, 55, 45, 58, 43, 52, 50, 59, 54, 49, 42, 44, 58, 37, 38, 42, 50,
    61, 67, 58, 63, 61, 56, 67, 59, 57, 61, 55,
)
STEP_OVERHEAD = 10


def route_tables(size):
    direct = np.full(size, 10**6)
    direct[0] = 0
    for distance, cost in zip(DISTANCES, STEP_COST):
        direct[distance] = direct[-distance % size] = cost + STEP_OVERHEAD
    cost, first = direct.copy(), np.arange(size)
    for step in range(1, size):
        by_two = direct[step] + np.roll(direct, step)
        first = np.where(by_two < cost, step, first)
        cost = np.minimum(cost, by_two)
    assert cost.max() < 10**6
    branch = np.zeros(size // 2 + 1, np.int32)
    branch[list(DISTANCES)] = np.arange(len(DISTANCES))
    table = np.zeros((3, size), np.int32)
    table[0], table[1], table[2, : branch.size] = cost, first, branch
    return table


def plan(peers, table, out):
    size = peers.shape[1]
    node = [peers[r, 0] for r in range(ROUNDS)]

    def wrapped(gap):
        return jnp.where(gap < 0, gap + size, gap)

    best = None
    for order in itertools.permutations(range(ROUNDS)):
        total, fields = None, []
        for place, r in enumerate(order):
            gap, onward = node[r], jnp.int32(0)
            if place:
                other = wrapped(node[r] - node[order[place - 1]])
                onward = jnp.where(table[0, other] < table[0, gap], 1, 0)
                gap = jnp.where(onward == 1, other, gap)
            total = table[0, gap] if total is None else total + table[0, gap]
            fields += [gap, onward]
        if best is None:
            best, kept = total, fields
        else:
            better = total < best
            best = jnp.where(better, total, best)
            kept = [jnp.where(better, n, o) for n, o in zip(fields, kept)]

    def emit(row, onward, gap, partner):
        out[FIELDS * row] = onward
        out[FIELDS * row + 1] = jnp.where(gap > size // 2, 1, 0)
        out[FIELDS * row + 2] = table[2, jnp.minimum(gap, size - gap)]
        out[FIELDS * row + 3] = partner

    row = jnp.int32(0)
    for r in range(ROUNDS):
        gap, onward = kept[2 * r], kept[2 * r + 1]
        step = table[1, gap]
        double = jnp.where(step == gap, 0, 1)
        emit(row, onward, step, jnp.where(double == 1, ROUNDS, r))
        emit(row + double, jnp.where(double == 1, 1, onward), wrapped(gap - step + step * (1 - double)), r)
        row = row + 1 + double
    emit(row, jnp.int32(0), jnp.int32(1), jnp.int32(ROUNDS))
    out[FIELDS * ROWS_OF_PLAN] = row


def start_kernel(
    peers, table, raw_pic, raw_cap,
    steps, count, first_branch, pic, cap, ahead, behind, pic_factor, cap_factor, pic_parts, cap_parts, losses,
    raw, unit, arrived, sent,
):
    loads = [pltpu.make_async_copy(src, raw.at[k], arrived.at[k]) for k, src in enumerate((raw_cap, raw_pic))]
    for load in loads:
        load.start()
    plan(peers, table, steps)
    count[0] = steps[FIELDS * ROWS_OF_PLAN]
    first_branch[0] = steps[2]
    swap = steps[1]
    for k, factor in enumerate((cap_factor, pic_factor)):
        loads[k].wait()
        wide = raw[k].astype(jnp.float32)
        scale = lax.rsqrt(jnp.sum(wide * wide, axis=-1, keepdims=True) + 1e-06)
        unit[k] = (wide * scale).astype(jnp.bfloat16)
        factor[...] = scale
    stores = [
        pltpu.make_async_copy(unit.at[place], out, sent.at[k])
        for k, (place, out) in enumerate(((swap, ahead), (1 - swap, behind), (0, cap), (1, pic)))
    ]
    for store in stores:
        store.start()
    for store in stores:
        store.wait()


def start(peers, pic, cap):
    rows, width = pic.shape
    smem = pl.BlockSpec(memory_space=pltpu.SMEM)
    vmem = pl.BlockSpec(memory_space=pltpu.VMEM)
    somewhere = pl.BlockSpec(memory_space=pl.ANY)
    unit = jax.ShapeDtypeStruct((rows, width), jnp.bfloat16)
    factor = jax.ShapeDtypeStruct((rows, 1), jnp.float32)
    parts = jax.ShapeDtypeStruct((ROUNDS, rows, width), jnp.bfloat16)
    fields = jax.ShapeDtypeStruct((FIELDS * ROWS_OF_PLAN + 1,), jnp.int32)
    return pl.pallas_call(
        start_kernel,
        out_shape=(
            fields, jax.ShapeDtypeStruct((1,), jnp.int32), jax.ShapeDtypeStruct((1,), jnp.int32), unit, unit, unit, unit, factor, factor, parts, parts,
            jax.ShapeDtypeStruct((ROUNDS, rows, LANES), jnp.float32),
        ),
        in_specs=[smem, smem, somewhere, somewhere],
        out_specs=(smem, smem, smem, *[somewhere] * 4, vmem, vmem, *[somewhere] * 3),
        scratch_shapes=[
            pltpu.VMEM((2, rows, width), jnp.bfloat16),
            pltpu.VMEM((2, rows, width), jnp.bfloat16),
            pltpu.SemaphoreType.DMA((2,)),
            pltpu.SemaphoreType.DMA((4,)),
        ],
        compiler_params=pltpu.CompilerParams(vmem_limit_bytes=START_VMEM_LIMIT),
        name="start",
    )(peers, jnp.asarray(route_tables(peers.shape[1])), pic, cap)


def shifted(x, by, size):
    return lax.ppermute(x, AXES, [(i, (i + by) % size) for i in range(size)])


def move(branch, ahead, behind, size):
    def mover(by):
        return lambda a, b: (shifted(b, by, size), shifted(a, -by, size))

    behind, ahead = lax.switch(branch, [mover(by) for by in DISTANCES], ahead, behind)
    return ahead, behind


def scores(left, right, sharp, shift):
    dots = lax.dot_general(left, right, (((1,), (1,)), ((), ())), preferred_element_type=jnp.float32)
    return sharp * dots + shift


def odds_ratio(odds):
    total = 1.0 + odds
    guess = pl.reciprocal(total, approx=True)
    return odds * (guess * (2.0 - total * guess))


def log_total(odds):
    return jnp.where(odds < 1e-3, odds - 0.5 * odds * odds, jnp.log(1.0 + odds))


def folded(wide):
    return sum(wide[:, k : k + LANES] for k in range(0, wide.shape[1], LANES))


def product(coeff, entries):
    return lax.dot_general(coeff, entries, (((1,), (0,)), ((), ())), preferred_element_type=jnp.float32)


def step_kernel(
    step, steps, sharp, shift, pic, cap, ahead, behind, old_pic_parts, old_cap_parts, old_losses,
    pic_parts, cap_parts, losses, next_ahead, next_behind, next_branch,
    held, part, loss, arrived, sent, kept,
):
    here = FIELDS * step[0]
    swap, partner = steps[here + 1], steps[here + 3]
    onward, next_swap = steps[here + 4], steps[here + 5]
    next_branch[0] = steps[here + 6]
    loads = [
        pltpu.make_async_copy(src, held.at[place], arrived.at[k])
        for k, (src, place) in enumerate(((ahead, 2 + swap), (behind, 3 - swap), (pic, 1), (cap, 0)))
    ]
    for load in loads:
        load.start()
    for load in loads:
        load.wait()
    stores = [
        pltpu.make_async_copy(held.at[2 * onward + place], out, sent.at[k])
        for k, (out, place) in enumerate(((next_ahead, next_swap), (next_behind, 1 - next_swap)))
    ]
    for store in stores:
        store.start()

    @pl.when(partner < ROUNDS)
    def _():
        keeps = []
        for k, (left, right, out) in enumerate(((1, 2, pic_parts), (0, 3, cap_parts))):
            for first in range(0, held.shape[1], HALF):
                rows = slice(first, first + HALF)
                odds = jnp.exp(scores(held[left, rows, :], held[right], sharp[0], shift[0]))
                coeff = (sharp[0] * odds_ratio(odds)).astype(jnp.bfloat16)
                if k == 0:
                    loss[rows, :] = folded(log_total(odds))
                part[k, rows, :] = product(coeff, held[right]).astype(jnp.bfloat16)
                keeps.append(
                    pltpu.make_async_copy(part.at[k, rows], out.at[partner, rows], kept.at[len(keeps)])
                )
                keeps[-1].start()
        keeps.append(pltpu.make_async_copy(loss, losses.at[partner], kept.at[len(keeps)]))
        keeps[-1].start()
        for keep in keeps:
            keep.wait()

    for store in stores:
        store.wait()


def last_kernel(
    mean_of, sharp, shift, pic, cap, pic_parts, cap_parts, losses, raw_pic, raw_cap, pic_factor, cap_factor,
    pic_grad, cap_grad, loss, held, raw, parts, lost, grads, arrived, sent,
):
    rows = held.shape[1]
    loads = [
        pltpu.make_async_copy(src, out, arrived.at[k])
        for k, (src, out) in enumerate((
            (pic, held.at[1]), (cap, held.at[0]), (pic_parts, parts.at[0]), (raw_pic, raw.at[0]),
            (cap_parts, parts.at[1]), (raw_cap, raw.at[1]), (losses, lost),
        ))
    ]
    for load in loads:
        load.start()
    loads[0].wait()
    loads[1].wait()
    columns_at = lax.broadcasted_iota(jnp.int32, (HALF, rows), 1)
    rows_at = lax.broadcasted_iota(jnp.int32, (HALF, rows), 0)
    stores, own_loss = [], []
    for side, (factor, grad) in enumerate(((pic_factor, pic_grad), (cap_factor, cap_grad))):
        for first in range(0, rows, HALF):
            here = slice(first, first + HALF)
            logits = scores(held[1 - side, here, :], held[side], sharp[0], shift[0])
            odds = jnp.exp(logits)
            label = jnp.where(rows_at + first == columns_at, 1.0, 0.0)
            if side == 0:
                own_loss.append(folded(log_total(odds) - label * logits))
            coeff = (sharp[0] * (odds_ratio(odds) - label)).astype(jnp.bfloat16)
            grads[side, here, :] = product(coeff, held[side])
            if first == 0:
                loads[2 + 2 * side].wait()
                loads[3 + 2 * side].wait()
            wide = raw[side, here, :].astype(jnp.float32)
            scale = factor[here, :]
            total = grads[side, here, :] + sum(parts[side, r, here, :].astype(jnp.float32) for r in range(ROUNDS))
            inner = jnp.sum(wide * total, axis=-1, keepdims=True)
            grads[side, here, :] = scale * total - wide * (scale * scale * scale * inner)
            stores.append(pltpu.make_async_copy(grads.at[side, here], grad.at[here], sent.at[len(stores)]))
            stores[-1].start()
    loads[6].wait()
    ones = jnp.full((8, LANES), 1.0, jnp.float32)
    total = lax.dot_general(
        ones, jnp.concatenate(own_loss, axis=0) + sum(lost[r] for r in range(ROUNDS)), (((1,), (1,)), ((), ())),
        precision=lax.Precision.HIGHEST, preferred_element_type=jnp.float32,
    )
    loss[...] = total[0:1, :] * (1.0 / mean_of)
    for store in stores:
        store.wait()


def step_tile(step, steps, sharp, shift, pic, cap, ahead, behind, *parts):
    rows, width = pic.shape
    smem = pl.BlockSpec(memory_space=pltpu.SMEM)
    somewhere = pl.BlockSpec(memory_space=pl.ANY)
    unit = jax.ShapeDtypeStruct((rows, width), jnp.bfloat16)
    return pl.pallas_call(
        step_kernel,
        out_shape=(
            *[jax.ShapeDtypeStruct(p.shape, p.dtype) for p in parts], unit, unit, jax.ShapeDtypeStruct((1,), jnp.int32)
        ),
        in_specs=[smem] * 4 + [somewhere] * 7,
        out_specs=(*[somewhere] * 5, smem),
        scratch_shapes=[
            pltpu.VMEM((4, rows, width), jnp.bfloat16),
            pltpu.VMEM((2, rows, width), jnp.bfloat16),
            pltpu.VMEM((rows, LANES), jnp.float32),
            pltpu.SemaphoreType.DMA((4,)),
            pltpu.SemaphoreType.DMA((2,)),
            pltpu.SemaphoreType.DMA((2 * rows // HALF + 1,)),
        ],
        input_output_aliases={8: 0, 9: 1, 10: 2},
        name="step_tile",
        compiler_params=pltpu.CompilerParams(vmem_limit_bytes=VMEM_LIMIT),
    )(step, steps, sharp, shift, pic, cap, ahead, behind, *parts)


def last_tile(mean_of, sharp, shift, pic, cap, parts, *rest):
    rows, width = pic.shape
    smem = pl.BlockSpec(memory_space=pltpu.SMEM)
    vmem = pl.BlockSpec(memory_space=pltpu.VMEM)
    somewhere = pl.BlockSpec(memory_space=pl.ANY)
    wide = jax.ShapeDtypeStruct((rows, width), jnp.float32)
    return pl.pallas_call(
        functools.partial(last_kernel, mean_of),
        out_shape=(wide, wide, jax.ShapeDtypeStruct((1, rows), jnp.float32)),
        in_specs=[smem, smem, *[somewhere] * 7, vmem, vmem],
        out_specs=(somewhere, somewhere, vmem),
        scratch_shapes=[
            pltpu.VMEM((2, rows, width), jnp.bfloat16),
            pltpu.VMEM((2, rows, width), jnp.bfloat16),
            pltpu.VMEM((2, ROUNDS, rows, width), jnp.bfloat16),
            pltpu.VMEM((ROUNDS, rows, LANES), jnp.float32),
            pltpu.VMEM((2, rows, width), jnp.float32),
            pltpu.SemaphoreType.DMA((7,)),
            pltpu.SemaphoreType.DMA((2 * rows // HALF,)),
        ],
        compiler_params=pltpu.CompilerParams(vmem_limit_bytes=VMEM_LIMIT),
        name="last_tile",
    )(sharp, shift, pic, cap, *parts, *rest)


def shards(picture_raw_features, caption_raw_features, peer_assignment, sharpness_factor, offset_term):
    size = peer_assignment.shape[1]
    rows = picture_raw_features.shape[0]
    steps, count, branch, pic, cap, ahead, behind, pic_factor, cap_factor, *parts = start(
        peer_assignment, picture_raw_features, caption_raw_features
    )
    scalars = sharpness_factor, offset_term

    def one_step(step, carry):
        branch, ahead, behind, *parts = carry
        ahead, behind = move(branch[0], ahead, behind, size)
        *parts, ahead, behind, branch = step_tile(step.reshape(1), steps, *scalars, pic, cap, ahead, behind, *parts)
        return branch, ahead, behind, *parts

    _, _, _, *parts = lax.fori_loop(0, count[0], one_step, (branch, ahead, behind, *parts))
    image_embedding_gradient, grad_text, row_loss = last_tile(
        (ROUNDS + 1) * rows, *scalars, pic, cap, parts, picture_raw_features, caption_raw_features, pic_factor, cap_factor
    )
    return image_embedding_gradient, grad_text, row_loss.reshape(rows)


def solution(mesh):
    placed = (P(AXES, None), P(AXES, None), P(), P(), P())
    return jax.shard_map(
        shards,
        mesh=mesh,
        in_specs=placed,
        out_specs=(P(AXES, None), P(AXES, None), P(AXES)),
        check_vma=False,
    )
```

```python
import functools
import itertools

import jax
import jax.numpy as jnp
import numpy as np
from jax import lax
from jax.experimental import pallas as pl
from jax.experimental.pallas import tpu as pltpu
from jax.sharding import PartitionSpec as P

AXES = ("gx", "gy")
HALF = 256
LANES = 128
FIELDS = 4
ROWS_OF_PLAN = 8
ROUNDS = 3
VMEM_LIMIT = 40 * 2**20
START_VMEM_LIMIT = 60 * 2**20

DISTANCES = (
    1, 3, 4, 5, 7, 8, 9, 10, 11, 13, 14, 15, 16, 17, 18, 19, 20, 21, 24, 25, 27, 28, 29, 30, 31, 32, 33, 36, 40, 42,
    43, 45, 53, 55, 56, 57, 59, 60, 61,
)
STEP_COST = (
    35, 39, 40, 49, 58, 58, 50, 61, 50, 43, 56, 38, 55, 45, 58, 43, 52, 50, 59, 54, 49, 42, 44, 58, 37, 38, 42, 50,
    61, 67, 58, 63, 61, 56, 67, 59, 57, 61, 55,
)
STEP_OVERHEAD = 10


def route_tables(size):
    direct = np.full(size, 10**6)
    direct[0] = 0
    for distance, cost in zip(DISTANCES, STEP_COST):
        direct[distance] = direct[-distance % size] = cost + STEP_OVERHEAD
    cost, first = direct.copy(), np.arange(size)
    for step in range(1, size):
        by_two = direct[step] + np.roll(direct, step)
        first = np.where(by_two < cost, step, first)
        cost = np.minimum(cost, by_two)
    assert cost.max() < 10**6
    branch = np.zeros(size // 2 + 1, np.int32)
    branch[list(DISTANCES)] = np.arange(len(DISTANCES))
    table = np.zeros((3, size), np.int32)
    table[0], table[1], table[2, : branch.size] = cost, first, branch
    return table


def plan(peers, table, out):
    size = peers.shape[1]
    node = [peers[r, 0] for r in range(ROUNDS)]

    def wrapped(gap):
        return jnp.where(gap < 0, gap + size, gap)

    best = None
    for order in itertools.permutations(range(ROUNDS)):
        total, fields = None, []
        for place, r in enumerate(order):
            gap, onward = node[r], jnp.int32(0)
            if place:
                other = wrapped(node[r] - node[order[place - 1]])
                onward = jnp.where(table[0, other] < table[0, gap], 1, 0)
                gap = jnp.where(onward == 1, other, gap)
            total = table[0, gap] if total is None else total + table[0, gap]
            fields += [gap, onward]
        if best is None:
            best, kept = total, fields
        else:
            better = total < best
            best = jnp.where(better, total, best)
            kept = [jnp.where(better, n, o) for n, o in zip(fields, kept)]

    def emit(row, onward, gap, partner):
        out[FIELDS * row] = onward
        out[FIELDS * row + 1] = jnp.where(gap > size // 2, 1, 0)
        out[FIELDS * row + 2] = table[2, jnp.minimum(gap, size - gap)]
        out[FIELDS * row + 3] = partner

    row = jnp.int32(0)
    for r in range(ROUNDS):
        gap, onward = kept[2 * r], kept[2 * r + 1]
        step = table[1, gap]
        double = jnp.where(step == gap, 0, 1)
        emit(row, onward, step, jnp.where(double == 1, ROUNDS, r))
        emit(row + double, jnp.where(double == 1, 1, onward), wrapped(gap - step + step * (1 - double)), r)
        row = row + 1 + double
    emit(row, jnp.int32(0), jnp.int32(1), jnp.int32(ROUNDS))
    out[FIELDS * ROWS_OF_PLAN] = row


def start_kernel(
    peers, table, raw_pic, raw_cap,
    steps, count, first_branch, pic, cap, ahead, behind, pic_factor, cap_factor, pic_parts, cap_parts, losses,
    raw, unit, arrived, sent,
):
    loads = [pltpu.make_async_copy(src, raw.at[k], arrived.at[k]) for k, src in enumerate((raw_cap, raw_pic))]
    for load in loads:
        load.start()
    plan(peers, table, steps)
    count[0] = steps[FIELDS * ROWS_OF_PLAN]
    first_branch[0] = steps[2]
    swap = steps[1]
    for k, factor in enumerate((cap_factor, pic_factor)):
        loads[k].wait()
        wide = raw[k].astype(jnp.float32)
        scale = lax.rsqrt(jnp.sum(wide * wide, axis=-1, keepdims=True) + 1e-06)
        unit[k] = (wide * scale).astype(jnp.bfloat16)
        factor[...] = scale
    stores = [
        pltpu.make_async_copy(unit.at[place], out, sent.at[k])
        for k, (place, out) in enumerate(((swap, ahead), (1 - swap, behind), (0, cap), (1, pic)))
    ]
    for store in stores:
        store.start()
    for store in stores:
        store.wait()


def start(peers, pic, cap):
    rows, width = pic.shape
    smem = pl.BlockSpec(memory_space=pltpu.SMEM)
    vmem = pl.BlockSpec(memory_space=pltpu.VMEM)
    somewhere = pl.BlockSpec(memory_space=pl.ANY)
    unit = jax.ShapeDtypeStruct((rows, width), jnp.bfloat16)
    factor = jax.ShapeDtypeStruct((rows, 1), jnp.float32)
    parts = jax.ShapeDtypeStruct((ROUNDS, rows, width), jnp.bfloat16)
    fields = jax.ShapeDtypeStruct((FIELDS * ROWS_OF_PLAN + 1,), jnp.int32)
    return pl.pallas_call(
        start_kernel,
        out_shape=(
            fields, jax.ShapeDtypeStruct((1,), jnp.int32), jax.ShapeDtypeStruct((1,), jnp.int32), unit, unit, unit, unit, factor, factor, parts, parts,
            jax.ShapeDtypeStruct((ROUNDS, rows, LANES), jnp.float32),
        ),
        in_specs=[smem, smem, somewhere, somewhere],
        out_specs=(smem, smem, smem, *[somewhere] * 4, vmem, vmem, *[somewhere] * 3),
        scratch_shapes=[
            pltpu.VMEM((2, rows, width), jnp.bfloat16),
            pltpu.VMEM((2, rows, width), jnp.bfloat16),
            pltpu.SemaphoreType.DMA((2,)),
            pltpu.SemaphoreType.DMA((4,)),
        ],
        compiler_params=pltpu.CompilerParams(vmem_limit_bytes=START_VMEM_LIMIT),
        name="start",
    )(peers, jnp.asarray(route_tables(peers.shape[1])), pic, cap)


def shifted(x, by, size):
    return lax.ppermute(x, AXES, [(i, (i + by) % size) for i in range(size)])


def move(branch, ahead, behind, size):
    def mover(by):
        return lambda a, b: (shifted(b, by, size), shifted(a, -by, size))

    behind, ahead = lax.switch(branch, [mover(by) for by in DISTANCES], ahead, behind)
    return ahead, behind


def scores(left, right, sharp, shift):
    dots = lax.dot_general(left, right, (((1,), (1,)), ((), ())), preferred_element_type=jnp.float32)
    return sharp * dots + shift


def odds_ratio(odds):
    total = 1.0 + odds
    guess = pl.reciprocal(total, approx=True)
    return odds * (guess * (2.0 - total * guess))


def log_total(odds):
    return jnp.where(odds < 1e-3, odds - 0.5 * odds * odds, jnp.log(1.0 + odds))


def folded(wide):
    return sum(wide[:, k : k + LANES] for k in range(0, wide.shape[1], LANES))


def product(coeff, entries):
    return lax.dot_general(coeff, entries, (((1,), (0,)), ((), ())), preferred_element_type=jnp.float32)


def step_kernel(
    step, steps, sharp, shift, pic, cap, ahead, behind, old_pic_parts, old_cap_parts, old_losses,
    pic_parts, cap_parts, losses, next_ahead, next_behind, next_branch,
    held, part, loss, arrived, sent, kept,
):
    here = FIELDS * step[0]
    swap, partner = steps[here + 1], steps[here + 3]
    onward, next_swap = steps[here + 4], steps[here + 5]
    next_branch[0] = steps[here + 6]
    loads = [
        pltpu.make_async_copy(src, held.at[place], arrived.at[k])
        for k, (src, place) in enumerate(((ahead, 2 + swap), (behind, 3 - swap), (pic, 1), (cap, 0)))
    ]
    for load in loads:
        load.start()
    for load in loads[:3]:
        load.wait()
    stores = [
        pltpu.make_async_copy(held.at[2 * onward + place], out, sent.at[k])
        for k, (out, place) in enumerate(((next_ahead, next_swap), (next_behind, 1 - next_swap)))
    ]

    @pl.when(partner < ROUNDS)
    def _():
        keeps = []
        for k, (left, right, out) in enumerate(((1, 2, pic_parts), (0, 3, cap_parts))):
            if k == 1:
                loads[3].wait()
                for store in stores:
                    store.start()
            odds = jnp.exp(scores(held[left], held[right], sharp[0], shift[0]))
            coeff = (sharp[0] * odds_ratio(odds)).astype(jnp.bfloat16)
            if k == 0:
                loss[...] = folded(log_total(odds))
            for first in range(0, held.shape[1], HALF):
                rows = slice(first, first + HALF)
                part[k, rows, :] = product(coeff[rows, :], held[right]).astype(jnp.bfloat16)
                keeps.append(
                    pltpu.make_async_copy(part.at[k, rows], out.at[partner, rows], kept.at[len(keeps)])
                )
                keeps[-1].start()
        keeps.append(pltpu.make_async_copy(loss, losses.at[partner], kept.at[len(keeps)]))
        keeps[-1].start()
        for keep in keeps:
            keep.wait()

    @pl.when(partner >= ROUNDS)
    def _():
        loads[3].wait()
        for store in stores:
            store.start()

    for store in stores:
        store.wait()


def last_kernel(
    mean_of, sharp, shift, pic, cap, pic_parts, cap_parts, losses, raw_pic, raw_cap, pic_factor, cap_factor,
    pic_grad, cap_grad, loss, held, raw, parts, lost, grads, arrived, sent,
):
    rows = held.shape[1]
    loads = [
        pltpu.make_async_copy(src, out, arrived.at[k])
        for k, (src, out) in enumerate((
            (pic, held.at[1]), (cap, held.at[0]), (pic_parts, parts.at[0]), (raw_pic, raw.at[0]),
            (cap_parts, parts.at[1]), (raw_cap, raw.at[1]), (losses, lost),
        ))
    ]
    for load in loads:
        load.start()
    loads[0].wait()
    loads[1].wait()
    columns_at = lax.broadcasted_iota(jnp.int32, (HALF, rows), 1)
    rows_at = lax.broadcasted_iota(jnp.int32, (HALF, rows), 0)
    stores, own_loss = [], []
    for side, (factor, grad) in enumerate(((pic_factor, pic_grad), (cap_factor, cap_grad))):
        for first in range(0, rows, HALF):
            here = slice(first, first + HALF)
            logits = scores(held[1 - side, here, :], held[side], sharp[0], shift[0])
            odds = jnp.exp(logits)
            label = jnp.where(rows_at + first == columns_at, 1.0, 0.0)
            if side == 0:
                own_loss.append(folded(log_total(odds) - label * logits))
            coeff = (sharp[0] * (odds_ratio(odds) - label)).astype(jnp.bfloat16)
            grads[side, here, :] = product(coeff, held[side])
            if first == 0:
                loads[2 + 2 * side].wait()
                loads[3 + 2 * side].wait()
            wide = raw[side, here, :].astype(jnp.float32)
            scale = factor[here, :]
            total = grads[side, here, :] + sum(parts[side, r, here, :].astype(jnp.float32) for r in range(ROUNDS))
            inner = jnp.sum(wide * total, axis=-1, keepdims=True)
            grads[side, here, :] = scale * total - wide * (scale * scale * scale * inner)
            stores.append(pltpu.make_async_copy(grads.at[side, here], grad.at[here], sent.at[len(stores)]))
            stores[-1].start()
    loads[6].wait()
    ones = jnp.full((8, LANES), 1.0, jnp.float32)
    total = lax.dot_general(
        ones, jnp.concatenate(own_loss, axis=0) + sum(lost[r] for r in range(ROUNDS)), (((1,), (1,)), ((), ())),
        precision=lax.Precision.HIGHEST, preferred_element_type=jnp.float32,
    )
    loss[...] = total[0:1, :] * (1.0 / mean_of)
    for store in stores:
        store.wait()


def step_tile(step, steps, sharp, shift, pic, cap, ahead, behind, *parts):
    rows, width = pic.shape
    smem = pl.BlockSpec(memory_space=pltpu.SMEM)
    somewhere = pl.BlockSpec(memory_space=pl.ANY)
    unit = jax.ShapeDtypeStruct((rows, width), jnp.bfloat16)
    return pl.pallas_call(
        step_kernel,
        out_shape=(
            *[jax.ShapeDtypeStruct(p.shape, p.dtype) for p in parts], unit, unit, jax.ShapeDtypeStruct((1,), jnp.int32)
        ),
        in_specs=[smem] * 4 + [somewhere] * 7,
        out_specs=(*[somewhere] * 5, smem),
        scratch_shapes=[
            pltpu.VMEM((4, rows, width), jnp.bfloat16),
            pltpu.VMEM((2, rows, width), jnp.bfloat16),
            pltpu.VMEM((rows, LANES), jnp.float32),
            pltpu.SemaphoreType.DMA((4,)),
            pltpu.SemaphoreType.DMA((2,)),
            pltpu.SemaphoreType.DMA((2 * rows // HALF + 1,)),
        ],
        input_output_aliases={8: 0, 9: 1, 10: 2},
        name="step_tile",
        compiler_params=pltpu.CompilerParams(vmem_limit_bytes=VMEM_LIMIT),
    )(step, steps, sharp, shift, pic, cap, ahead, behind, *parts)


def last_tile(mean_of, sharp, shift, pic, cap, parts, *rest):
    rows, width = pic.shape
    smem = pl.BlockSpec(memory_space=pltpu.SMEM)
    vmem = pl.BlockSpec(memory_space=pltpu.VMEM)
    somewhere = pl.BlockSpec(memory_space=pl.ANY)
    wide = jax.ShapeDtypeStruct((rows, width), jnp.float32)
    return pl.pallas_call(
        functools.partial(last_kernel, mean_of),
        out_shape=(wide, wide, jax.ShapeDtypeStruct((1, rows), jnp.float32)),
        in_specs=[smem, smem, *[somewhere] * 7, vmem, vmem],
        out_specs=(somewhere, somewhere, vmem),
        scratch_shapes=[
            pltpu.VMEM((2, rows, width), jnp.bfloat16),
            pltpu.VMEM((2, rows, width), jnp.bfloat16),
            pltpu.VMEM((2, ROUNDS, rows, width), jnp.bfloat16),
            pltpu.VMEM((ROUNDS, rows, LANES), jnp.float32),
            pltpu.VMEM((2, rows, width), jnp.float32),
            pltpu.SemaphoreType.DMA((7,)),
            pltpu.SemaphoreType.DMA((2 * rows // HALF,)),
        ],
        compiler_params=pltpu.CompilerParams(vmem_limit_bytes=VMEM_LIMIT),
        name="last_tile",
    )(sharp, shift, pic, cap, *parts, *rest)


def shards(picture_raw_features, caption_raw_features, peer_assignment, sharpness_factor, offset_term):
    size = peer_assignment.shape[1]
    rows = picture_raw_features.shape[0]
    steps, count, branch, pic, cap, ahead, behind, pic_factor, cap_factor, *parts = start(
        peer_assignment, picture_raw_features, caption_raw_features
    )
    scalars = sharpness_factor, offset_term

    def one_step(step, carry):
        branch, ahead, behind, *parts = carry
        ahead, behind = move(branch[0], ahead, behind, size)
        *parts, ahead, behind, branch = step_tile(step.reshape(1), steps, *scalars, pic, cap, ahead, behind, *parts)
        return branch, ahead, behind, *parts

    _, _, _, *parts = lax.fori_loop(0, count[0], one_step, (branch, ahead, behind, *parts))
    image_embedding_gradient, grad_text, row_loss = last_tile(
        (ROUNDS + 1) * rows, *scalars, pic, cap, parts, picture_raw_features, caption_raw_features, pic_factor, cap_factor
    )
    return image_embedding_gradient, grad_text, row_loss.reshape(rows)


def solution(mesh):
    placed = (P(AXES, None), P(AXES, None), P(), P(), P())
    return jax.shard_map(
        shards,
        mesh=mesh,
        in_specs=placed,
        out_specs=(P(AXES, None), P(AXES, None), P(AXES)),
        check_vma=False,
    )
```

```python
import functools
import itertools

import jax
import jax.numpy as jnp
import numpy as np
from jax import lax
from jax.experimental import pallas as pl
from jax.experimental.pallas import tpu as pltpu
from jax.sharding import PartitionSpec as P

AXES = ("gx", "gy")
HALF = 256
LANES = 128
FIELDS = 4
ROWS_OF_PLAN = 8
ROUNDS = 3
VMEM_LIMIT = 40 * 2**20
START_VMEM_LIMIT = 60 * 2**20

DISTANCES = (
    1, 3, 4, 5, 7, 8, 9, 10, 11, 13, 14, 15, 16, 17, 18, 19, 20, 21, 24, 25, 27, 28, 29, 30, 31, 32, 33, 36, 40, 42,
    43, 45, 53, 55, 56, 57, 59, 60, 61,
)
STEP_COST = (
    35, 39, 40, 49, 58, 58, 50, 61, 50, 43, 56, 38, 55, 45, 58, 43, 52, 50, 59, 54, 49, 42, 44, 58, 37, 38, 42, 50,
    61, 67, 58, 63, 61, 56, 67, 59, 57, 61, 55,
)
STEP_OVERHEAD = 10


def route_tables(size):
    direct = np.full(size, 10**6)
    direct[0] = 0
    for distance, cost in zip(DISTANCES, STEP_COST):
        direct[distance] = direct[-distance % size] = cost + STEP_OVERHEAD
    cost, first = direct.copy(), np.arange(size)
    for step in range(1, size):
        by_two = direct[step] + np.roll(direct, step)
        first = np.where(by_two < cost, step, first)
        cost = np.minimum(cost, by_two)
    assert cost.max() < 10**6
    branch = np.zeros(size // 2 + 1, np.int32)
    branch[list(DISTANCES)] = np.arange(len(DISTANCES))
    table = np.zeros((3, size), np.int32)
    table[0], table[1], table[2, : branch.size] = cost, first, branch
    return table


def plan(peers, table, out):
    size = peers.shape[1]
    node = [peers[r, 0] for r in range(ROUNDS)]

    def wrapped(gap):
        return jnp.where(gap < 0, gap + size, gap)

    best = None
    for order in itertools.permutations(range(ROUNDS)):
        total, fields = None, []
        for place, r in enumerate(order):
            gap, onward = node[r], jnp.int32(0)
            if place:
                other = wrapped(node[r] - node[order[place - 1]])
                onward = jnp.where(table[0, other] < table[0, gap], 1, 0)
                gap = jnp.where(onward == 1, other, gap)
            total = table[0, gap] if total is None else total + table[0, gap]
            fields += [gap, onward]
        if best is None:
            best, kept = total, fields
        else:
            better = total < best
            best = jnp.where(better, total, best)
            kept = [jnp.where(better, n, o) for n, o in zip(fields, kept)]

    def emit(row, onward, gap, partner):
        out[FIELDS * row] = onward
        out[FIELDS * row + 1] = jnp.where(gap > size // 2, 1, 0)
        out[FIELDS * row + 2] = table[2, jnp.minimum(gap, size - gap)]
        out[FIELDS * row + 3] = partner

    row = jnp.int32(0)
    for r in range(ROUNDS):
        gap, onward = kept[2 * r], kept[2 * r + 1]
        step = table[1, gap]
        double = jnp.where(step == gap, 0, 1)
        emit(row, onward, step, jnp.where(double == 1, ROUNDS, r))
        emit(row + double, jnp.where(double == 1, 1, onward), wrapped(gap - step + step * (1 - double)), r)
        row = row + 1 + double
    emit(row, jnp.int32(0), jnp.int32(1), jnp.int32(ROUNDS))
    out[FIELDS * ROWS_OF_PLAN] = row


def start_kernel(
    peers, table, raw_pic, raw_cap,
    steps, count, first_branch, pic, cap, ahead, behind, pic_factor, cap_factor, pic_parts, cap_parts, losses,
    raw, unit, arrived, sent,
):
    loads = [pltpu.make_async_copy(src, raw.at[k], arrived.at[k]) for k, src in enumerate((raw_cap, raw_pic))]
    for load in loads:
        load.start()
    plan(peers, table, steps)
    count[0] = steps[FIELDS * ROWS_OF_PLAN]
    first_branch[0] = steps[2]
    swap = steps[1]
    for k, factor in enumerate((cap_factor, pic_factor)):
        loads[k].wait()
        wide = raw[k].astype(jnp.float32)
        scale = lax.rsqrt(jnp.sum(wide * wide, axis=-1, keepdims=True) + 1e-06)
        unit[k] = (wide * scale).astype(jnp.bfloat16)
        factor[...] = scale
    stores = [
        pltpu.make_async_copy(unit.at[place], out, sent.at[k])
        for k, (place, out) in enumerate(((swap, ahead), (1 - swap, behind), (0, cap), (1, pic)))
    ]
    for store in stores:
        store.start()
    for store in stores:
        store.wait()


def start(peers, pic, cap):
    rows, width = pic.shape
    smem = pl.BlockSpec(memory_space=pltpu.SMEM)
    vmem = pl.BlockSpec(memory_space=pltpu.VMEM)
    somewhere = pl.BlockSpec(memory_space=pl.ANY)
    unit = jax.ShapeDtypeStruct((rows, width), jnp.bfloat16)
    factor = jax.ShapeDtypeStruct((rows, 1), jnp.float32)
    parts = jax.ShapeDtypeStruct((ROUNDS, rows, width), jnp.bfloat16)
    fields = jax.ShapeDtypeStruct((FIELDS * ROWS_OF_PLAN + 1,), jnp.int32)
    return pl.pallas_call(
        start_kernel,
        out_shape=(
            fields, jax.ShapeDtypeStruct((1,), jnp.int32), jax.ShapeDtypeStruct((1,), jnp.int32), unit, unit, unit, unit, factor, factor, parts, parts,
            jax.ShapeDtypeStruct((ROUNDS, rows, LANES), jnp.float32),
        ),
        in_specs=[smem, smem, somewhere, somewhere],
        out_specs=(smem, smem, smem, *[somewhere] * 4, vmem, vmem, *[somewhere] * 3),
        scratch_shapes=[
            pltpu.VMEM((2, rows, width), jnp.bfloat16),
            pltpu.VMEM((2, rows, width), jnp.bfloat16),
            pltpu.SemaphoreType.DMA((2,)),
            pltpu.SemaphoreType.DMA((4,)),
        ],
        compiler_params=pltpu.CompilerParams(vmem_limit_bytes=START_VMEM_LIMIT),
        name="start",
    )(peers, jnp.asarray(route_tables(peers.shape[1])), pic, cap)


def shifted(x, by, size):
    return lax.ppermute(x, AXES, [(i, (i + by) % size) for i in range(size)])


def move(branch, ahead, behind, size):
    def mover(by):
        return lambda a, b: (shifted(b, by, size), shifted(a, -by, size))

    behind, ahead = lax.switch(branch, [mover(by) for by in DISTANCES], ahead, behind)
    return ahead, behind


def scores(left, right, sharp, shift):
    dots = lax.dot_general(left, right, (((1,), (1,)), ((), ())), preferred_element_type=jnp.float32)
    return sharp * dots + shift


def odds_ratio(odds):
    total = 1.0 + odds
    guess = pl.reciprocal(total, approx=True)
    return odds * (guess * (2.0 - total * guess))


def log_total(odds):
    return jnp.where(odds < 1e-3, odds - 0.5 * odds * odds, jnp.log(1.0 + odds))


def folded(wide):
    return sum(wide[:, k : k + LANES] for k in range(0, wide.shape[1], LANES))


def product(coeff, entries):
    return lax.dot_general(coeff, entries, (((1,), (0,)), ((), ())), preferred_element_type=jnp.float32)


def step_kernel(
    step, steps, sharp, shift, pic, cap, ahead, behind, old_pic_parts, old_cap_parts, old_losses,
    pic_parts, cap_parts, losses, next_ahead, next_behind, next_branch,
    held, part, loss, arrived, sent, kept,
):
    here = FIELDS * step[0]
    swap, partner = steps[here + 1], steps[here + 3]
    onward, next_swap = steps[here + 4], steps[here + 5]
    next_branch[0] = steps[here + 6]
    loads = [
        pltpu.make_async_copy(src, held.at[place], arrived.at[k])
        for k, (src, place) in enumerate(((ahead, 2 + swap), (behind, 3 - swap), (pic, 1), (cap, 0)))
    ]
    for load in loads:
        load.start()
    for load in loads[:3]:
        load.wait()
    stores = [
        pltpu.make_async_copy(held.at[2 * onward + place], out, sent.at[k])
        for k, (out, place) in enumerate(((next_ahead, next_swap), (next_behind, 1 - next_swap)))
    ]

    @pl.when(partner < ROUNDS)
    def _():
        keeps = []
        for k, (left, right, out) in enumerate(((1, 2, pic_parts), (0, 3, cap_parts))):
            if k == 1:
                loads[3].wait()
                for store in stores:
                    store.start()
            odds = jnp.exp(scores(held[left], held[right], sharp[0], shift[0]))
            coeff = (sharp[0] * odds_ratio(odds)).astype(jnp.bfloat16)
            if k == 0:
                loss[...] = folded(log_total(odds))
            for first in range(0, held.shape[1], HALF):
                rows = slice(first, first + HALF)
                part[k, rows, :] = product(coeff[rows, :], held[right]).astype(jnp.bfloat16)
                keeps.append(
                    pltpu.make_async_copy(part.at[k, rows], out.at[partner, rows], kept.at[len(keeps)])
                )
                keeps[-1].start()
        keeps.append(pltpu.make_async_copy(loss, losses.at[partner], kept.at[len(keeps)]))
        keeps[-1].start()
        for keep in keeps:
            keep.wait()

    @pl.when(partner >= ROUNDS)
    def _():
        loads[3].wait()
        for store in stores:
            store.start()

    for store in stores:
        store.wait()


def last_kernel(
    mean_of, sharp, shift, pic, cap, pic_parts, cap_parts, losses, raw_pic, raw_cap, pic_factor, cap_factor,
    pic_grad, cap_grad, loss, held, raw, parts, lost, grads, arrived, sent,
):
    rows = held.shape[1]
    loads = [
        pltpu.make_async_copy(src, out, arrived.at[k])
        for k, (src, out) in enumerate((
            (pic, held.at[1]), (cap, held.at[0]), (pic_parts, parts.at[0]), (raw_pic, raw.at[0]),
            (cap_parts, parts.at[1]), (raw_cap, raw.at[1]), (losses, lost),
        ))
    ]
    for load in loads:
        load.start()
    loads[0].wait()
    loads[1].wait()
    columns_at = lax.broadcasted_iota(jnp.int32, (rows, rows), 1)
    rows_at = lax.broadcasted_iota(jnp.int32, (rows, rows), 0)
    stores, own_loss = [], []
    for side, (factor, grad) in enumerate(((pic_factor, pic_grad), (cap_factor, cap_grad))):
        logits = scores(held[1 - side], held[side], sharp[0], shift[0])
        odds = jnp.exp(logits)
        label = jnp.where(rows_at == columns_at, 1.0, 0.0)
        if side == 0:
            own_loss.append(folded(log_total(odds) - label * logits))
        coeff = (sharp[0] * (odds_ratio(odds) - label)).astype(jnp.bfloat16)
        for first in range(0, rows, HALF):
            here = slice(first, first + HALF)
            grads[side, here, :] = product(coeff[here, :], held[side])
            if first == 0:
                loads[2 + 2 * side].wait()
                loads[3 + 2 * side].wait()
            wide = raw[side, here, :].astype(jnp.float32)
            scale = factor[here, :]
            total = grads[side, here, :] + sum(parts[side, r, here, :].astype(jnp.float32) for r in range(ROUNDS))
            inner = jnp.sum(wide * total, axis=-1, keepdims=True)
            grads[side, here, :] = scale * total - wide * (scale * scale * scale * inner)
            stores.append(pltpu.make_async_copy(grads.at[side, here], grad.at[here], sent.at[len(stores)]))
            stores[-1].start()
    loads[6].wait()
    ones = jnp.full((8, LANES), 1.0, jnp.float32)
    total = lax.dot_general(
        ones, jnp.concatenate(own_loss, axis=0) + sum(lost[r] for r in range(ROUNDS)), (((1,), (1,)), ((), ())),
        precision=lax.Precision.HIGHEST, preferred_element_type=jnp.float32,
    )
    loss[...] = total[0:1, :] * (1.0 / mean_of)
    for store in stores:
        store.wait()


def step_tile(step, steps, sharp, shift, pic, cap, ahead, behind, *parts):
    rows, width = pic.shape
    smem = pl.BlockSpec(memory_space=pltpu.SMEM)
    somewhere = pl.BlockSpec(memory_space=pl.ANY)
    unit = jax.ShapeDtypeStruct((rows, width), jnp.bfloat16)
    return pl.pallas_call(
        step_kernel,
        out_shape=(
            *[jax.ShapeDtypeStruct(p.shape, p.dtype) for p in parts], unit, unit, jax.ShapeDtypeStruct((1,), jnp.int32)
        ),
        in_specs=[smem] * 4 + [somewhere] * 7,
        out_specs=(*[somewhere] * 5, smem),
        scratch_shapes=[
            pltpu.VMEM((4, rows, width), jnp.bfloat16),
            pltpu.VMEM((2, rows, width), jnp.bfloat16),
            pltpu.VMEM((rows, LANES), jnp.float32),
            pltpu.SemaphoreType.DMA((4,)),
            pltpu.SemaphoreType.DMA((2,)),
            pltpu.SemaphoreType.DMA((2 * rows // HALF + 1,)),
        ],
        input_output_aliases={8: 0, 9: 1, 10: 2},
        name="step_tile",
        compiler_params=pltpu.CompilerParams(vmem_limit_bytes=VMEM_LIMIT),
    )(step, steps, sharp, shift, pic, cap, ahead, behind, *parts)


def last_tile(mean_of, sharp, shift, pic, cap, parts, *rest):
    rows, width = pic.shape
    smem = pl.BlockSpec(memory_space=pltpu.SMEM)
    vmem = pl.BlockSpec(memory_space=pltpu.VMEM)
    somewhere = pl.BlockSpec(memory_space=pl.ANY)
    wide = jax.ShapeDtypeStruct((rows, width), jnp.float32)
    return pl.pallas_call(
        functools.partial(last_kernel, mean_of),
        out_shape=(wide, wide, jax.ShapeDtypeStruct((1, rows), jnp.float32)),
        in_specs=[smem, smem, *[somewhere] * 7, vmem, vmem],
        out_specs=(somewhere, somewhere, vmem),
        scratch_shapes=[
            pltpu.VMEM((2, rows, width), jnp.bfloat16),
            pltpu.VMEM((2, rows, width), jnp.bfloat16),
            pltpu.VMEM((2, ROUNDS, rows, width), jnp.bfloat16),
            pltpu.VMEM((ROUNDS, rows, LANES), jnp.float32),
            pltpu.VMEM((2, rows, width), jnp.float32),
            pltpu.SemaphoreType.DMA((7,)),
            pltpu.SemaphoreType.DMA((2 * rows // HALF,)),
        ],
        compiler_params=pltpu.CompilerParams(vmem_limit_bytes=VMEM_LIMIT),
        name="last_tile",
    )(sharp, shift, pic, cap, *parts, *rest)


def shards(picture_raw_features, caption_raw_features, peer_assignment, sharpness_factor, offset_term):
    size = peer_assignment.shape[1]
    rows = picture_raw_features.shape[0]
    steps, count, branch, pic, cap, ahead, behind, pic_factor, cap_factor, *parts = start(
        peer_assignment, picture_raw_features, caption_raw_features
    )
    scalars = sharpness_factor, offset_term

    def one_step(step, carry):
        branch, ahead, behind, *parts = carry
        ahead, behind = move(branch[0], ahead, behind, size)
        *parts, ahead, behind, branch = step_tile(step.reshape(1), steps, *scalars, pic, cap, ahead, behind, *parts)
        return branch, ahead, behind, *parts

    _, _, _, *parts = lax.fori_loop(0, count[0], one_step, (branch, ahead, behind, *parts))
    image_embedding_gradient, grad_text, row_loss = last_tile(
        (ROUNDS + 1) * rows, *scalars, pic, cap, parts, picture_raw_features, caption_raw_features, pic_factor, cap_factor
    )
    return image_embedding_gradient, grad_text, row_loss.reshape(rows)


def solution(mesh):
    placed = (P(AXES, None), P(AXES, None), P(), P(), P())
    return jax.shard_map(
        shards,
        mesh=mesh,
        in_specs=placed,
        out_specs=(P(AXES, None), P(AXES, None), P(AXES)),
        check_vma=False,
    )
```
